128 devices in a mesh: lat: 8 (over y, core), elev: 16 (over z, x).
Axes of the slice: x: 4, y: 4, z: 4, core: 2. Of those that a mesh axis runs over, the one named last changes fastest.
Arguments:
- frames: float32 [512, 512, 2048], P('lat', 'elev')
- start_basis: float32 [512, 96], replicated, may hold values from -6 to 6
Outputs:
- core: float32 [512, 96, 2048], P('lat', None, 'elev')
- basis: float32 [512, 96], P('elev')
The draws below stay inside these ranges and needn't reach their ends.
All inputs are finite; a program needn't handle non-finite values.
Results may differ from the reference program's by a relative error of at most 0.00024.
Values sent between devices are 32-bit elements; how exact they have to be, the bound alone decides.
A program may use at most 192 MiB of HBM per device.

```python
import jax
import jax.numpy as jnp
from jax import lax

R = 128
L = 512
E = 512
K = 96
F = 16
ITERS = 3


def draw_frames(key, part):
    key = jax.random.fold_in(key, 11)
    keys = jax.random.split(key, 12)
    scale = jnp.exp(jax.random.uniform(keys[0], (1, E, 1), jnp.float32, jnp.log(0.5), jnp.log(2.0)))
    noise = jax.random.normal(keys[1], (L, E, F * R), jnp.float32)
    total = noise * scale
    for comp in range(4):
        common = jax.random.normal(keys[2 + comp], (L, 1, F * R), jnp.float32)
        profile = jax.random.uniform(keys[6 + comp], (1, E, 1), jnp.float32, -0.4, 0.4)
        total = total + common * profile
    return total


def centred(rng, shape, deviation, most, dtype=jnp.bfloat16):
    array = jax.random.normal(rng, shape, jnp.float32) * deviation
    return jnp.minimum(jnp.maximum(array, -most), most).astype(dtype)


def setup_inputs(seed: int = 0) -> dict:
    key_of = jax.random.split(jax.random.key(seed), 3)
    return {
        "frames": draw_frames(jax.random.fold_in(key_of[2], 71), 0),
        "start_basis": centred(key_of[1], (E, K), 1.0, 6.0, jnp.float32),
    }


def orth_once(w):
    c = jnp.linalg.cholesky(jnp.dot(w.T, w, precision=lax.Precision.HIGHEST))
    return lax.linalg.triangular_solve(c, w, left_side=False, lower=True, transpose_a=True)

def orth(w):
    return orth_once(orth_once(w))

def reference(frames, start_basis):

    def step(total, block):
        part = jnp.dot(block, block.T, precision=lax.Precision.HIGHEST)
        return (total + part, None)
    gram, _ = lax.scan(step, jnp.zeros((E, E), jnp.float32), frames)
    basis = start_basis
    for turn in range(ITERS):
        basis = orth(jnp.dot(gram, basis, precision=lax.Precision.HIGHEST))
    core = jnp.einsum('lec,ek->lkc', frames, basis, precision=lax.Precision.HIGHEST)
    return (core, basis)
```

```python
import functools

import jax
import jax.numpy as jnp
from jax import lax
from jax.experimental import pallas as pl
from jax.experimental.pallas import tpu as pltpu
from jax.sharding import PartitionSpec as P

ITERS = 3
HIGHEST = lax.Precision.HIGHEST
LANES = 128
STEP = 4
Z = 4
X = 4


def orth_once(w):
    c = jnp.linalg.cholesky(jnp.dot(w.T, w, precision=HIGHEST))
    return lax.linalg.triangular_solve(c, w, left_side=False, lower=True, transpose_a=True)


def orth(w):
    return orth_once(orth_once(w))


def dot_nt(a, b):
    return lax.dot_general(
        a, b, (((1,), (1,)), ((), ())), precision=HIGHEST, preferred_element_type=jnp.float32
    )


def gather_gram_kernel(
    frames, x_out, g_out, buf, gacc, packed, half_in, half, ring_in, part, y_in, total, half_all,
    recv, send, own_sem, ar_recv, ar_send, out_sem,
):
    lines = frames.shape[0]
    own = frames.shape[1]
    chunks = lines // STEP
    lat = lax.axis_index("lat")
    elev = lax.axis_index("elev")
    core = lax.rem(lat, 2)
    y = lat // 2
    x = lax.rem(elev, X)
    z = elev // X
    partner = lat + 1 - 2 * core
    peers = []
    for dz in range(Z):
        for dx in range(X):
            if dz or dx:
                peers.append(lax.rem(z + dz, Z) * X + lax.rem(x + dx, X))
    y_peers = [lax.rem(y + dy, 4) * 2 + core for dy in range(1, 4)]

    barrier = pltpu.get_barrier_semaphore()
    for p in peers:
        pl.semaphore_signal(barrier, inc=1, device_id={"elev": p}, device_id_type=pl.DeviceIdType.MESH)
    for q in y_peers + [partner]:
        pl.semaphore_signal(barrier, inc=1, device_id={"lat": q}, device_id_type=pl.DeviceIdType.MESH)
    pl.semaphore_wait(barrier, len(peers) + len(y_peers) + 1)

    gacc[...] = jnp.zeros_like(gacc)
    mine = pl.ds(pl.multiple_of(elev * own, own), own)

    def issue(c, _):
        rows = pl.ds(c * STEP, STEP)
        for p in peers:
            pltpu.make_async_remote_copy(
                src_ref=frames.at[rows, :, pl.ds(pl.multiple_of(p * LANES, LANES), LANES)],
                dst_ref=buf.at[rows, mine, :],
                send_sem=send.at[c],
                recv_sem=recv.at[c],
                device_id={"elev": p},
                device_id_type=pl.DeviceIdType.MESH,
            ).start()
        pltpu.make_async_copy(
            frames.at[rows, :, pl.ds(pl.multiple_of(elev * LANES, LANES), LANES)],
            buf.at[rows, mine, :],
            recv.at[c],
        ).start()
        return 0

    lax.fori_loop(0, chunks, issue, 0)

    def consume(c, _):
        rows = pl.ds(c * STEP, STEP)
        pltpu.make_async_copy(buf.at[rows], buf.at[rows], recv.at[c]).wait()
        pltpu.make_async_copy(buf.at[rows], x_out.at[rows], out_sem.at[c]).start()
        block = jnp.concatenate([buf[c * STEP + i] for i in range(STEP)], axis=1)
        low, high = block[:256], block[256:]
        gacc[0] += dot_nt(low, low)
        gacc[1] += dot_nt(high, low)
        gacc[2] += dot_nt(high, high)
        return 0

    lax.fori_loop(0, chunks, consume, 0)

    places = [(0, 0, 0), (0, 1, 0), (0, 1, 1), (1, 0, 0), (1, 0, 1), (1, 1, 0), (1, 1, 1), (2, 0, 0), (2, 1, 0), (2, 1, 1)]
    for n, (g, i, j) in enumerate(places):
        packed[pl.ds(n * 128, 128), :] = gacc[g, pl.ds(i * 128, 128), pl.ds(j * 128, 128)]

    hrows = half.shape[0]
    srows = part.shape[0]
    copy = pltpu.make_async_remote_copy(
        src_ref=packed.at[pl.ds(pl.multiple_of((1 - core) * hrows, 8), hrows), :],
        dst_ref=half_in,
        send_sem=ar_send.at[0],
        recv_sem=ar_recv.at[0],
        device_id={"lat": partner},
        device_id_type=pl.DeviceIdType.MESH,
    )
    copy.start()
    copy.wait()
    half[...] = packed[pl.ds(pl.multiple_of(core * hrows, 8), hrows), :] + half_in[...]
    for p in peers:
        pltpu.make_async_remote_copy(
            src_ref=half.at[pl.ds(pl.multiple_of(p * srows, 8), srows), :],
            dst_ref=ring_in.at[elev],
            send_sem=ar_send.at[1],
            recv_sem=ar_recv.at[1],
            device_id={"elev": p},
            device_id_type=pl.DeviceIdType.MESH,
        ).start()
    pltpu.make_async_copy(
        half.at[pl.ds(pl.multiple_of(elev * srows, 8), srows), :], ring_in.at[elev], ar_recv.at[1]
    ).start()
    pltpu.make_async_copy(ring_in, ring_in, ar_recv.at[1]).wait()
    acc = ring_in[0]
    for i in range(1, Z * X):
        acc = acc + ring_in[i]
    part[...] = acc
    for q in y_peers:
        pltpu.make_async_remote_copy(
            src_ref=part,
            dst_ref=y_in.at[y],
            send_sem=ar_send.at[2],
            recv_sem=ar_recv.at[2],
            device_id={"lat": q},
            device_id_type=pl.DeviceIdType.MESH,
        ).start()
    pltpu.make_async_copy(part, y_in.at[y], ar_recv.at[2]).start()
    pltpu.make_async_copy(y_in, y_in, ar_recv.at[2]).wait()
    total[...] = (y_in[0] + y_in[1]) + (y_in[2] + y_in[3])
    place = pl.ds(pl.multiple_of(elev * srows, 8), srows)
    for p in peers:
        pltpu.make_async_remote_copy(
            src_ref=total,
            dst_ref=half_all.at[place, :],
            send_sem=ar_send.at[3],
            recv_sem=ar_recv.at[3],
            device_id={"elev": p},
            device_id_type=pl.DeviceIdType.MESH,
        ).start()
    pltpu.make_async_copy(total, half_all.at[place, :], ar_recv.at[3]).start()
    pltpu.make_async_copy(half_all, half_all, ar_recv.at[3]).wait()
    spot = pl.ds(pl.multiple_of(core * hrows, 8), hrows)
    copy = pltpu.make_async_remote_copy(
        src_ref=half_all,
        dst_ref=g_out.at[spot, :],
        send_sem=ar_send.at[4],
        recv_sem=ar_recv.at[4],
        device_id={"lat": partner},
        device_id_type=pl.DeviceIdType.MESH,
    )
    copy.start()
    g_out[spot, :] = half_all[...]
    copy.wait()

    n = Z * X - 1
    pltpu.make_async_copy(half.at[pl.ds(0, n * srows), :], half.at[pl.ds(0, n * srows), :], ar_send.at[1]).wait()
    pltpu.make_async_copy(y_in.at[pl.ds(0, 3)], y_in.at[pl.ds(0, 3)], ar_send.at[2]).wait()
    pltpu.make_async_copy(half.at[pl.ds(0, n * srows), :], half.at[pl.ds(0, n * srows), :], ar_send.at[3]).wait()

    def drain(c, _):
        rows = pl.ds(c * STEP, STEP)
        gone = buf.at[rows, pl.ds(0, n * own), :]
        pltpu.make_async_copy(gone, gone, send.at[c]).wait()
        pltpu.make_async_copy(buf.at[rows], x_out.at[rows], out_sem.at[c]).wait()
        return 0

    lax.fori_loop(0, chunks, drain, 0)


def gather_gram(frames):
    lines, own, columns = frames.shape
    elevs = own * Z * X
    chunks = lines // STEP
    rows = 1280
    return pl.pallas_call(
        gather_gram_kernel,
        out_shape=(
            jax.ShapeDtypeStruct((lines, elevs, LANES), jnp.float32),
            jax.ShapeDtypeStruct((rows, LANES), jnp.float32),
        ),
        in_specs=[pl.BlockSpec(memory_space=pl.ANY)],
        out_specs=(pl.BlockSpec(memory_space=pl.ANY), pl.BlockSpec(memory_space=pltpu.VMEM)),
        scratch_shapes=[
            pltpu.VMEM((lines, elevs, LANES), jnp.float32),
            pltpu.VMEM((3, 256, 256), jnp.float32),
            pltpu.VMEM((rows, LANES), jnp.float32),
            pltpu.VMEM((rows // 2, LANES), jnp.float32),
            pltpu.VMEM((rows // 2, LANES), jnp.float32),
            pltpu.VMEM((16, rows // 32, LANES), jnp.float32),
            pltpu.VMEM((rows // 32, LANES), jnp.float32),
            pltpu.VMEM((4, rows // 32, LANES), jnp.float32),
            pltpu.VMEM((rows // 32, LANES), jnp.float32),
            pltpu.VMEM((rows // 2, LANES), jnp.float32),
            pltpu.SemaphoreType.DMA((chunks,)),
            pltpu.SemaphoreType.DMA((chunks,)),
            pltpu.SemaphoreType.DMA((1,)),
            pltpu.SemaphoreType.DMA((5,)),
            pltpu.SemaphoreType.DMA((5,)),
            pltpu.SemaphoreType.DMA((chunks,)),
        ],
        compiler_params=pltpu.CompilerParams(
            collective_id=0, has_side_effects=True, vmem_limit_bytes=48 * 1024 * 1024
        ),
        cost_estimate=pl.CostEstimate(
            flops=2 * lines * LANES * elevs * elevs, bytes_accessed=3 * frames.size * 4, transcendentals=0
        ),
        name="gather_gram",
    )(frames)


def unpack(packed):
    b = packed.reshape(10, 128, 128)
    t = [x.T for x in b]
    return jnp.concatenate(
        [
            jnp.concatenate([b[0], t[1], t[3], t[5]], axis=1),
            jnp.concatenate([b[1], b[2], t[4], t[6]], axis=1),
            jnp.concatenate([b[3], b[4], b[7], t[8]], axis=1),
            jnp.concatenate([b[5], b[6], b[8], b[9]], axis=1),
        ],
        axis=0,
    )


def per_device(frames, start_basis):
    regrouped, packed = gather_gram(frames)
    gram = unpack(packed)
    basis = start_basis
    for turn in range(ITERS):
        basis = orth(jnp.dot(gram, basis, precision=HIGHEST))
    core = jnp.einsum("lec,ek->lkc", regrouped, basis, precision=HIGHEST)
    own_count = frames.shape[1]
    own_basis = lax.dynamic_slice_in_dim(basis, lax.axis_index("elev") * own_count, own_count, 0)
    return (core, own_basis)


def solution(mesh):
    return jax.shard_map(
        per_device,
        mesh=mesh,
        in_specs=(P("lat", "elev", None), P()),
        out_specs=(P("lat", None, "elev"), P("elev", None)),
        check_vma=False,
    )
```

```python
import functools

import jax
import jax.numpy as jnp
from jax import lax
from jax.experimental import pallas as pl
from jax.experimental.pallas import tpu as pltpu
from jax.sharding import PartitionSpec as P

ITERS = 3
HIGHEST = lax.Precision.HIGHEST
LANES = 128
STEP = 4
Z = 4
X = 4


def dot_nt(a, b):
    return lax.dot_general(
        a, b, (((1,), (1,)), ((), ())), precision=HIGHEST, preferred_element_type=jnp.float32
    )


def gather_gram_kernel(
    frames, x_out, g_out, buf, gacc, packed, half_in, half, ring_in, part, y_in, total, half_all,
    recv, send, ar_recv, ar_send, out_sem,
):
    lines = frames.shape[0]
    own = frames.shape[1]
    chunks = lines // STEP
    lat = lax.axis_index("lat")
    elev = lax.axis_index("elev")
    core = lax.rem(lat, 2)
    y = lat // 2
    x = lax.rem(elev, X)
    z = elev // X
    partner = lat + 1 - 2 * core
    peers = []
    for dz in range(Z):
        for dx in range(X):
            if dz or dx:
                peers.append(lax.rem(z + dz, Z) * X + lax.rem(x + dx, X))
    y_peers = [lax.rem(y + dy, 4) * 2 + core for dy in range(1, 4)]

    barrier = pltpu.get_barrier_semaphore()
    for p in peers:
        pl.semaphore_signal(barrier, inc=1, device_id={"elev": p}, device_id_type=pl.DeviceIdType.MESH)
    for q in y_peers + [partner]:
        pl.semaphore_signal(barrier, inc=1, device_id={"lat": q}, device_id_type=pl.DeviceIdType.MESH)
    pl.semaphore_wait(barrier, len(peers) + len(y_peers) + 1)

    gacc[...] = jnp.zeros_like(gacc)
    mine = pl.ds(pl.multiple_of(elev * own, own), own)

    def issue(c, _):
        rows = pl.ds(c * STEP, STEP)
        for p in peers:
            pltpu.make_async_remote_copy(
                src_ref=frames.at[rows, :, pl.ds(pl.multiple_of(p * LANES, LANES), LANES)],
                dst_ref=buf.at[rows, mine, :],
                send_sem=send.at[c],
                recv_sem=recv.at[c],
                device_id={"elev": p},
                device_id_type=pl.DeviceIdType.MESH,
            ).start()
        pltpu.make_async_copy(
            frames.at[rows, :, pl.ds(pl.multiple_of(elev * LANES, LANES), LANES)],
            buf.at[rows, mine, :],
            recv.at[c],
        ).start()
        return 0

    lax.fori_loop(0, chunks, issue, 0)

    def consume(c, _):
        rows = pl.ds(c * STEP, STEP)
        pltpu.make_async_copy(buf.at[rows], buf.at[rows], recv.at[c]).wait()
        pltpu.make_async_copy(buf.at[rows], x_out.at[rows], out_sem.at[c]).start()
        block = jnp.concatenate([buf[c * STEP + i] for i in range(STEP)], axis=1)
        low, high = block[:256], block[256:]
        gacc[0] += dot_nt(low, low)
        gacc[1] += dot_nt(high, low)
        gacc[2] += dot_nt(high, high)
        return 0

    lax.fori_loop(0, chunks, consume, 0)

    places = [(0, 0, 0), (0, 1, 0), (0, 1, 1), (1, 0, 0), (1, 0, 1), (1, 1, 0), (1, 1, 1), (2, 0, 0), (2, 1, 0), (2, 1, 1)]
    for n, (g, i, j) in enumerate(places):
        packed[pl.ds(n * 128, 128), :] = gacc[g, pl.ds(i * 128, 128), pl.ds(j * 128, 128)]

    hrows = half.shape[0]
    srows = part.shape[0]
    copy = pltpu.make_async_remote_copy(
        src_ref=packed.at[pl.ds(pl.multiple_of((1 - core) * hrows, 8), hrows), :],
        dst_ref=half_in,
        send_sem=ar_send.at[0],
        recv_sem=ar_recv.at[0],
        device_id={"lat": partner},
        device_id_type=pl.DeviceIdType.MESH,
    )
    copy.start()
    copy.wait()
    half[...] = packed[pl.ds(pl.multiple_of(core * hrows, 8), hrows), :] + half_in[...]
    for p in peers:
        pltpu.make_async_remote_copy(
            src_ref=half.at[pl.ds(pl.multiple_of(p * srows, 8), srows), :],
            dst_ref=ring_in.at[elev],
            send_sem=ar_send.at[1],
            recv_sem=ar_recv.at[1],
            device_id={"elev": p},
            device_id_type=pl.DeviceIdType.MESH,
        ).start()
    pltpu.make_async_copy(
        half.at[pl.ds(pl.multiple_of(elev * srows, 8), srows), :], ring_in.at[elev], ar_recv.at[1]
    ).start()
    pltpu.make_async_copy(ring_in, ring_in, ar_recv.at[1]).wait()
    acc = ring_in[0]
    for i in range(1, Z * X):
        acc = acc + ring_in[i]
    part[...] = acc
    for q in y_peers:
        pltpu.make_async_remote_copy(
            src_ref=part,
            dst_ref=y_in.at[y],
            send_sem=ar_send.at[2],
            recv_sem=ar_recv.at[2],
            device_id={"lat": q},
            device_id_type=pl.DeviceIdType.MESH,
        ).start()
    pltpu.make_async_copy(part, y_in.at[y], ar_recv.at[2]).start()
    pltpu.make_async_copy(y_in, y_in, ar_recv.at[2]).wait()
    total[...] = (y_in[0] + y_in[1]) + (y_in[2] + y_in[3])
    place = pl.ds(pl.multiple_of(elev * srows, 8), srows)
    for p in peers:
        pltpu.make_async_remote_copy(
            src_ref=total,
            dst_ref=half_all.at[place, :],
            send_sem=ar_send.at[3],
            recv_sem=ar_recv.at[3],
            device_id={"elev": p},
            device_id_type=pl.DeviceIdType.MESH,
        ).start()
    pltpu.make_async_copy(total, half_all.at[place, :], ar_recv.at[3]).start()
    pltpu.make_async_copy(half_all, half_all, ar_recv.at[3]).wait()
    spot = pl.ds(pl.multiple_of(core * hrows, 8), hrows)
    copy = pltpu.make_async_remote_copy(
        src_ref=half_all,
        dst_ref=g_out.at[spot, :],
        send_sem=ar_send.at[4],
        recv_sem=ar_recv.at[4],
        device_id={"lat": partner},
        device_id_type=pl.DeviceIdType.MESH,
    )
    copy.start()
    g_out[spot, :] = half_all[...]
    copy.wait()

    n = Z * X - 1
    pltpu.make_async_copy(half.at[pl.ds(0, n * srows), :], half.at[pl.ds(0, n * srows), :], ar_send.at[1]).wait()
    pltpu.make_async_copy(y_in.at[pl.ds(0, 3)], y_in.at[pl.ds(0, 3)], ar_send.at[2]).wait()
    pltpu.make_async_copy(half.at[pl.ds(0, n * srows), :], half.at[pl.ds(0, n * srows), :], ar_send.at[3]).wait()

    def drain(c, _):
        rows = pl.ds(c * STEP, STEP)
        gone = buf.at[rows, pl.ds(0, n * own), :]
        pltpu.make_async_copy(gone, gone, send.at[c]).wait()
        pltpu.make_async_copy(buf.at[rows], x_out.at[rows], out_sem.at[c]).wait()
        return 0

    lax.fori_loop(0, chunks, drain, 0)


def gather_gram(frames):
    lines, own, columns = frames.shape
    elevs = own * Z * X
    chunks = lines // STEP
    rows = 1280
    return pl.pallas_call(
        gather_gram_kernel,
        out_shape=(
            jax.ShapeDtypeStruct((lines, elevs, LANES), jnp.float32),
            jax.ShapeDtypeStruct((rows, LANES), jnp.float32),
        ),
        in_specs=[pl.BlockSpec(memory_space=pl.ANY)],
        out_specs=(pl.BlockSpec(memory_space=pl.ANY), pl.BlockSpec(memory_space=pltpu.VMEM)),
        scratch_shapes=[
            pltpu.VMEM((lines, elevs, LANES), jnp.float32),
            pltpu.VMEM((3, 256, 256), jnp.float32),
            pltpu.VMEM((rows, LANES), jnp.float32),
            pltpu.VMEM((rows // 2, LANES), jnp.float32),
            pltpu.VMEM((rows // 2, LANES), jnp.float32),
            pltpu.VMEM((16, rows // 32, LANES), jnp.float32),
            pltpu.VMEM((rows // 32, LANES), jnp.float32),
            pltpu.VMEM((4, rows // 32, LANES), jnp.float32),
            pltpu.VMEM((rows // 32, LANES), jnp.float32),
            pltpu.VMEM((rows // 2, LANES), jnp.float32),
            pltpu.SemaphoreType.DMA((chunks,)),
            pltpu.SemaphoreType.DMA((chunks,)),
            pltpu.SemaphoreType.DMA((5,)),
            pltpu.SemaphoreType.DMA((5,)),
            pltpu.SemaphoreType.DMA((chunks,)),
        ],
        compiler_params=pltpu.CompilerParams(
            collective_id=0, has_side_effects=True, vmem_limit_bytes=48 * 1024 * 1024
        ),
        cost_estimate=pl.CostEstimate(
            flops=2 * lines * LANES * elevs * elevs, bytes_accessed=3 * frames.size * 4, transcendentals=0
        ),
        name="gather_gram",
    )(frames)


def iota(shape, dim):
    return lax.broadcasted_iota(jnp.int32, shape, dim)


def dot_nn(a, b):
    return jnp.dot(a, b, precision=HIGHEST, preferred_element_type=jnp.float32)


def split(v):
    high = v.astype(jnp.bfloat16)
    return high, (v - high.astype(jnp.float32)).astype(jnp.bfloat16)


def cholesky_inverse(m):
    n = m.shape[0]
    tiles = n // 8
    sub, lane = iota((8, n), 0), iota((8, n), 1)

    def up(row):
        return jnp.broadcast_to(row, (8, n))

    a = [m[8 * i : 8 * i + 8, :] for i in range(tiles)]
    v = [jnp.where(lane == sub + 8 * i, 1.0, 0.0) for i in range(tiles)]
    out = []
    for p in range(tiles):
        j = 8 * p
        c = [[jnp.broadcast_to(a[i][:, j + t : j + t + 1], (8, n)) for i in range(p, tiles)] for t in range(8)]
        factors = []
        for t in range(8):
            inverse = 1.0 / up(c[t][0][t : t + 1, :])
            f = [q * inverse for q in c[t]]
            f[0] = jnp.where(sub > t, f[0], 0.0)
            factors.append(f)
            for s in range(t + 1, 8):
                scale = up(c[t][0][s : s + 1, :])
                c[s] = [q - g * scale for q, g in zip(c[s], f)]
        pivots = c[0][0]
        for t in range(1, 8):
            pivots = jnp.where(sub == t, c[t][0], pivots)
        for t in range(8):
            ra, rv = up(a[p][t : t + 1, :]), up(v[p][t : t + 1, :])
            a[p] = a[p] - factors[t][0] * ra
            v[p] = v[p] - factors[t][0] * rv
        for t in range(8):
            ra, rv = up(a[p][t : t + 1, :]), up(v[p][t : t + 1, :])
            for i in range(p + 1, tiles):
                a[i] = a[i] - factors[t][i - p] * ra
                v[i] = v[i] - factors[t][i - p] * rv
        out.append(v[p] * lax.rsqrt(pivots))
    return jnp.concatenate(out, axis=0)


def near_identity_inverse(m):
    n = m.shape[0]
    row, column = iota((n, n), 0), iota((n, n), 1)
    eye = jnp.where(row == column, 1.0, 0.0)
    e = m - eye
    short = eye - jnp.where(row > column, e, jnp.where(row == column, 0.5 * e, 0.0))
    return lax.cond(jnp.sum(e * e) <= 3e-8, lambda: short, lambda: cholesky_inverse(m))


def basis_core_kernel(x, packed, start, core, basis_out, buf, gram, out, turned, in_sem, out_sem):
    chunks = x.shape[0] // STEP

    def load(c):
        rows = pl.ds(c * STEP, STEP)
        return pltpu.make_async_copy(x.at[rows], buf.at[rows], in_sem.at[c])

    def store(c):
        rows = pl.ds(c * STEP, STEP)
        return pltpu.make_async_copy(out.at[rows], core.at[rows], out_sem.at[c])

    for c in range(chunks):
        load(c).start()

    places = [(0, 0), (1, 0), (1, 1), (2, 0), (2, 1), (3, 0), (3, 1), (2, 2), (3, 2), (3, 3)]
    for n, (i, j) in enumerate(places):
        tile = packed[pl.ds(n * 128, 128), :]
        gram[pl.ds(i * 128, 128), pl.ds(j * 128, 128)] = tile
        if i != j:
            gram[pl.ds(j * 128, 128), pl.ds(i * 128, 128)] = tile.T

    def turn(_, b):
        w = dot_nn(b, gram[...])
        w = dot_nn(cholesky_inverse(dot_nt(w, w)), w)
        return dot_nn(near_identity_inverse(dot_nt(w, w)), w)

    basis = lax.fori_loop(0, ITERS, turn, start[...].T)
    turned[...] = basis.T
    own = basis_out.shape[0]
    basis_out[...] = turned[pl.ds(pl.multiple_of(lax.axis_index("elev") * own, 8), own), :]

    high, low = split(basis)
    both = jnp.concatenate([high, low], axis=0)
    kept = basis.shape[0]

    def project(c, _):
        load(c).wait()
        for i in range(0, STEP, 2):
            l = c * STEP + i
            xh, xl = split(jnp.concatenate([buf[l], buf[l + 1]], axis=1))
            r = jnp.dot(both, xh, preferred_element_type=jnp.float32)
            q = jnp.dot(high, xl, preferred_element_type=jnp.float32)
            s = r[:kept] + (r[kept:] + q)
            out[l] = s[:, :LANES]
            out[l + 1] = s[:, LANES:]
        store(c).start()
        return 0

    lax.fori_loop(0, chunks, project, 0)

    def drain(c, _):
        store(c).wait()
        return 0

    lax.fori_loop(0, chunks, drain, 0)


def basis_core(x, packed, start, own):
    lines, elevs, lanes = x.shape
    kept = start.shape[1]
    chunks = lines // STEP
    return pl.pallas_call(
        basis_core_kernel,
        out_shape=(
            jax.ShapeDtypeStruct((lines, kept, lanes), jnp.float32),
            jax.ShapeDtypeStruct((own, kept), jnp.float32),
        ),
        in_specs=[pl.BlockSpec(memory_space=pl.ANY)] + [pl.BlockSpec(memory_space=pltpu.VMEM)] * 2,
        out_specs=(pl.BlockSpec(memory_space=pl.ANY), pl.BlockSpec(memory_space=pltpu.VMEM)),
        scratch_shapes=[
            pltpu.VMEM((lines, elevs, lanes), jnp.float32),
            pltpu.VMEM((elevs, elevs), jnp.float32),
            pltpu.VMEM((lines, kept, lanes), jnp.float32),
            pltpu.VMEM((elevs, kept), jnp.float32),
            pltpu.SemaphoreType.DMA((chunks,)),
            pltpu.SemaphoreType.DMA((chunks,)),
        ],
        compiler_params=pltpu.CompilerParams(vmem_limit_bytes=48 * 1024 * 1024),
        cost_estimate=pl.CostEstimate(
            flops=6 * lines * lanes * elevs * kept, bytes_accessed=2 * x.size * 4, transcendentals=0
        ),
        name="basis_core",
    )(x, packed, start)


def per_device(frames, start_basis):
    regrouped, packed = gather_gram(frames)
    return basis_core(regrouped, packed, start_basis, frames.shape[1])


def solution(mesh):
    return jax.shard_map(
        per_device,
        mesh=mesh,
        in_specs=(P("lat", "elev", None), P()),
        out_specs=(P("lat", None, "elev"), P("elev", None)),
        check_vma=False,
    )
```

```python
import functools

import jax
import jax.numpy as jnp
from jax import lax
from jax.experimental import pallas as pl
from jax.experimental.pallas import tpu as pltpu
from jax.sharding import PartitionSpec as P

ITERS = 3
HIGHEST = lax.Precision.HIGHEST
LANES = 128
STEP = 2
CORE_STEP = 16
Z = 4
X = 4


def dot_nt(a, b):
    return lax.dot_general(
        a, b, (((1,), (1,)), ((), ())), precision=HIGHEST, preferred_element_type=jnp.float32
    )


def hops(offset):
    return min(offset[0], Z - offset[0]) + min(offset[1], X - offset[1])


def gather_gram_kernel(
    frames, x_out, g_out, buf, gacc, packed, half_in, half, ring_in, part, y_in, total, half_all,
    recv, send, ar_recv, ar_send, out_sem,
):
    lines = frames.shape[0]
    own = frames.shape[1]
    chunks = lines // STEP
    lat = lax.axis_index("lat")
    elev = lax.axis_index("elev")
    core = lax.rem(lat, 2)
    y = lat // 2
    x = lax.rem(elev, X)
    z = elev // X
    partner = lat + 1 - 2 * core
    offsets = sorted([(dz, dx) for dz in range(Z) for dx in range(X) if dz or dx], key=hops)
    far_first = [lax.rem(z + dz, Z) * X + lax.rem(x + dx, X) for dz, dx in reversed(offsets)]
    peers = []
    for n in range(len(far_first)):
        peers.append(far_first[n // 2] if n % 2 else far_first[len(far_first) - 1 - n // 2])
    y_peers = [lax.rem(y + dy, 4) * 2 + core for dy in (2, 1, 3)]

    barrier = pltpu.get_barrier_semaphore()
    for p in peers:
        pl.semaphore_signal(barrier, inc=1, device_id={"elev": p}, device_id_type=pl.DeviceIdType.MESH)
    for q in y_peers + [partner]:
        pl.semaphore_signal(barrier, inc=1, device_id={"lat": q}, device_id_type=pl.DeviceIdType.MESH)
    pl.semaphore_wait(barrier, len(peers) + len(y_peers) + 1)

    gacc[...] = jnp.zeros_like(gacc)
    mine = pl.ds(pl.multiple_of(elev * own, own), own)

    def issue(c, _):
        rows = pl.ds(c * STEP, STEP)
        for p in peers:
            pltpu.make_async_remote_copy(
                src_ref=frames.at[rows, :, pl.ds(pl.multiple_of(p * LANES, LANES), LANES)],
                dst_ref=buf.at[rows, mine, :],
                send_sem=send.at[c],
                recv_sem=recv.at[c],
                device_id={"elev": p},
                device_id_type=pl.DeviceIdType.MESH,
            ).start()
        pltpu.make_async_copy(
            frames.at[rows, :, pl.ds(pl.multiple_of(elev * LANES, LANES), LANES)],
            buf.at[rows, mine, :],
            recv.at[c],
        ).start()
        return 0

    lax.fori_loop(0, chunks, issue, 0)

    def consume(c, _):
        rows = pl.ds(c * STEP, STEP)
        pltpu.make_async_copy(buf.at[rows], buf.at[rows], recv.at[c]).wait()
        pltpu.make_async_copy(buf.at[rows], x_out.at[rows], out_sem.at[c]).start()
        block = jnp.concatenate([buf[c * STEP + i] for i in range(STEP)], axis=1)
        low, high = block[:256], block[256:]
        gacc[0] += dot_nt(low, low)
        gacc[1] += dot_nt(high, low)
        gacc[2] += dot_nt(high, high)
        return 0

    lax.fori_loop(0, chunks, consume, 0)

    places = [(0, 0, 0), (0, 1, 0), (0, 1, 1), (1, 0, 0), (1, 0, 1), (1, 1, 0), (1, 1, 1), (2, 0, 0), (2, 1, 0), (2, 1, 1)]
    for n, (g, i, j) in enumerate(places):
        packed[pl.ds(n * 128, 128), :] = gacc[g, pl.ds(i * 128, 128), pl.ds(j * 128, 128)]

    hrows = half.shape[0]
    srows = part.shape[0]
    copy = pltpu.make_async_remote_copy(
        src_ref=packed.at[pl.ds(pl.multiple_of((1 - core) * hrows, 8), hrows), :],
        dst_ref=half_in,
        send_sem=ar_send.at[0],
        recv_sem=ar_recv.at[0],
        device_id={"lat": partner},
        device_id_type=pl.DeviceIdType.MESH,
    )
    copy.start()
    copy.wait()
    half[...] = packed[pl.ds(pl.multiple_of(core * hrows, 8), hrows), :] + half_in[...]
    for p in far_first:
        pltpu.make_async_remote_copy(
            src_ref=half.at[pl.ds(pl.multiple_of(p * srows, 8), srows), :],
            dst_ref=ring_in.at[elev],
            send_sem=ar_send.at[1],
            recv_sem=ar_recv.at[1],
            device_id={"elev": p},
            device_id_type=pl.DeviceIdType.MESH,
        ).start()
    pltpu.make_async_copy(
        half.at[pl.ds(pl.multiple_of(elev * srows, 8), srows), :], ring_in.at[elev], ar_recv.at[1]
    ).start()
    pltpu.make_async_copy(ring_in, ring_in, ar_recv.at[1]).wait()
    acc = ring_in[0]
    for i in range(1, Z * X):
        acc = acc + ring_in[i]
    part[...] = acc
    for q in y_peers:
        pltpu.make_async_remote_copy(
            src_ref=part,
            dst_ref=y_in.at[y],
            send_sem=ar_send.at[2],
            recv_sem=ar_recv.at[2],
            device_id={"lat": q},
            device_id_type=pl.DeviceIdType.MESH,
        ).start()
    pltpu.make_async_copy(part, y_in.at[y], ar_recv.at[2]).start()
    pltpu.make_async_copy(y_in, y_in, ar_recv.at[2]).wait()
    total[...] = (y_in[0] + y_in[1]) + (y_in[2] + y_in[3])
    place = pl.ds(pl.multiple_of(elev * srows, 8), srows)
    for p in far_first:
        pltpu.make_async_remote_copy(
            src_ref=total,
            dst_ref=half_all.at[place, :],
            send_sem=ar_send.at[3],
            recv_sem=ar_recv.at[3],
            device_id={"elev": p},
            device_id_type=pl.DeviceIdType.MESH,
        ).start()
    pltpu.make_async_copy(total, half_all.at[place, :], ar_recv.at[3]).start()
    pltpu.make_async_copy(half_all, half_all, ar_recv.at[3]).wait()
    spot = pl.ds(pl.multiple_of(core * hrows, 8), hrows)
    copy = pltpu.make_async_remote_copy(
        src_ref=half_all,
        dst_ref=g_out.at[spot, :],
        send_sem=ar_send.at[4],
        recv_sem=ar_recv.at[4],
        device_id={"lat": partner},
        device_id_type=pl.DeviceIdType.MESH,
    )
    copy.start()
    g_out[spot, :] = half_all[...]
    copy.wait()

    n = Z * X - 1
    pltpu.make_async_copy(half.at[pl.ds(0, n * srows), :], half.at[pl.ds(0, n * srows), :], ar_send.at[1]).wait()
    pltpu.make_async_copy(y_in.at[pl.ds(0, 3)], y_in.at[pl.ds(0, 3)], ar_send.at[2]).wait()
    pltpu.make_async_copy(half.at[pl.ds(0, n * srows), :], half.at[pl.ds(0, n * srows), :], ar_send.at[3]).wait()

    def drain(c, _):
        rows = pl.ds(c * STEP, STEP)
        gone = buf.at[rows, pl.ds(0, n * own), :]
        pltpu.make_async_copy(gone, gone, send.at[c]).wait()
        pltpu.make_async_copy(buf.at[rows], x_out.at[rows], out_sem.at[c]).wait()
        return 0

    lax.fori_loop(0, chunks, drain, 0)


def gather_gram(frames):
    lines, own, columns = frames.shape
    elevs = own * Z * X
    chunks = lines // STEP
    rows = 1280
    return pl.pallas_call(
        gather_gram_kernel,
        out_shape=(
            jax.ShapeDtypeStruct((lines, elevs, LANES), jnp.float32),
            jax.ShapeDtypeStruct((rows, LANES), jnp.float32),
        ),
        in_specs=[pl.BlockSpec(memory_space=pl.ANY)],
        out_specs=(pl.BlockSpec(memory_space=pl.ANY), pl.BlockSpec(memory_space=pltpu.VMEM)),
        scratch_shapes=[
            pltpu.VMEM((lines, elevs, LANES), jnp.float32),
            pltpu.VMEM((3, 256, 256), jnp.float32),
            pltpu.VMEM((rows, LANES), jnp.float32),
            pltpu.VMEM((rows // 2, LANES), jnp.float32),
            pltpu.VMEM((rows // 2, LANES), jnp.float32),
            pltpu.VMEM((16, rows // 32, LANES), jnp.float32),
            pltpu.VMEM((rows // 32, LANES), jnp.float32),
            pltpu.VMEM((4, rows // 32, LANES), jnp.float32),
            pltpu.VMEM((rows // 32, LANES), jnp.float32),
            pltpu.VMEM((rows // 2, LANES), jnp.float32),
            pltpu.SemaphoreType.DMA((chunks,)),
            pltpu.SemaphoreType.DMA((chunks,)),
            pltpu.SemaphoreType.DMA((5,)),
            pltpu.SemaphoreType.DMA((5,)),
            pltpu.SemaphoreType.DMA((chunks,)),
        ],
        compiler_params=pltpu.CompilerParams(
            collective_id=0, has_side_effects=True, vmem_limit_bytes=48 * 1024 * 1024
        ),
        cost_estimate=pl.CostEstimate(
            flops=2 * lines * LANES * elevs * elevs, bytes_accessed=3 * frames.size * 4, transcendentals=0
        ),
        name="gather_gram",
    )(frames)


def iota(shape, dim):
    return lax.broadcasted_iota(jnp.int32, shape, dim)


def dot_nn(a, b):
    return jnp.dot(a, b, precision=HIGHEST, preferred_element_type=jnp.float32)


def split(v):
    high = v.astype(jnp.bfloat16)
    return high, (v - high.astype(jnp.float32)).astype(jnp.bfloat16)


def cholesky_inverse(m):
    n = m.shape[0]
    tiles = n // 8
    sub, lane = iota((8, n), 0), iota((8, n), 1)

    def up(row):
        return jnp.broadcast_to(row, (8, n))

    a = [m[8 * i : 8 * i + 8, :] for i in range(tiles)]
    v = [jnp.where(lane == sub + 8 * i, 1.0, 0.0) for i in range(tiles)]
    out = []
    for p in range(tiles):
        j = 8 * p
        c = [[jnp.broadcast_to(a[i][:, j + t : j + t + 1], (8, n)) for i in range(p, tiles)] for t in range(8)]
        factors = []
        for t in range(8):
            inverse = 1.0 / up(c[t][0][t : t + 1, :])
            f = [q * inverse for q in c[t]]
            f[0] = jnp.where(sub > t, f[0], 0.0)
            factors.append(f)
            for s in range(t + 1, 8):
                scale = up(c[t][0][s : s + 1, :])
                c[s] = [q - g * scale for q, g in zip(c[s], f)]
        pivots = c[0][0]
        for t in range(1, 8):
            pivots = jnp.where(sub == t, c[t][0], pivots)
        for t in range(8):
            ra, rv = up(a[p][t : t + 1, :]), up(v[p][t : t + 1, :])
            a[p] = a[p] - factors[t][0] * ra
            v[p] = v[p] - factors[t][0] * rv
        for t in range(8):
            ra, rv = up(a[p][t : t + 1, :]), up(v[p][t : t + 1, :])
            for i in range(p + 1, tiles):
                a[i] = a[i] - factors[t][i - p] * ra
                v[i] = v[i] - factors[t][i - p] * rv
        out.append(v[p] * lax.rsqrt(pivots))
    return jnp.concatenate(out, axis=0)


def orth_again(w):
    m = dot_nt(w, w)
    row, column = iota(m.shape, 0), iota(m.shape, 1)
    e = m - jnp.where(row == column, 1.0, 0.0)
    lower = jnp.where(row > column, e, jnp.where(row == column, 0.5 * e, 0.0))
    return lax.cond(
        jnp.sum(e * e) <= 3e-8,
        lambda: w - jnp.dot(lower.astype(jnp.bfloat16), w.astype(jnp.bfloat16), preferred_element_type=jnp.float32),
        lambda: dot_nn(cholesky_inverse(m), w),
    )


def basis_core_kernel(x, packed, start, core, basis_out, buf, first, gram, out, turned, in_sem, start_sem, out_sem):
    chunks = x.shape[0] // CORE_STEP

    def load(c):
        rows = pl.ds(c * CORE_STEP, CORE_STEP)
        return pltpu.make_async_copy(x.at[rows], buf.at[rows], in_sem.at[c])

    def store(c):
        rows = pl.ds(c * CORE_STEP, CORE_STEP)
        return pltpu.make_async_copy(out.at[rows], core.at[rows], out_sem.at[c])

    begin = pltpu.make_async_copy(start, first, start_sem)
    begin.start()
    for c in range(chunks):
        load(c).start()

    places = [(0, 0), (1, 0), (1, 1), (2, 0), (2, 1), (3, 0), (3, 1), (2, 2), (3, 2), (3, 3)]
    for n, (i, j) in enumerate(places):
        tile = packed[pl.ds(n * 128, 128), :]
        gram[pl.ds(i * 128, 128), pl.ds(j * 128, 128)] = tile
        if i != j:
            gram[pl.ds(j * 128, 128), pl.ds(i * 128, 128)] = tile.T

    def turn(_, b):
        w = dot_nn(b, gram[...])
        w = dot_nn(cholesky_inverse(dot_nt(w, w)), w)
        return orth_again(w)

    begin.wait()
    basis = lax.fori_loop(0, ITERS, turn, first[...])
    turned[...] = basis.T
    own = basis_out.shape[0]
    basis_out[...] = turned[pl.ds(pl.multiple_of(lax.axis_index("elev") * own, 8), own), :]

    high, low = split(basis)
    both = jnp.concatenate([high, low], axis=0)
    kept = basis.shape[0]

    for c in range(chunks):
        load(c).wait()

    def project(c, _):
        for i in range(0, CORE_STEP, 2):
            l = c * CORE_STEP + i
            xh, xl = split(jnp.concatenate([buf[l], buf[l + 1]], axis=1))
            r = jnp.dot(both, xh, preferred_element_type=jnp.float32)
            q = jnp.dot(high, xl, preferred_element_type=jnp.float32)
            s = r[:kept] + (r[kept:] + q)
            out[l] = s[:, :LANES]
            out[l + 1] = s[:, LANES:]
        store(c).start()
        return 0

    lax.fori_loop(0, chunks, project, 0)

    def drain(c, _):
        store(c).wait()
        return 0

    lax.fori_loop(0, chunks, drain, 0)


def basis_core(x, packed, start, own):
    lines, elevs, lanes = x.shape
    kept = start.shape[0]
    chunks = lines // CORE_STEP
    return pl.pallas_call(
        basis_core_kernel,
        out_shape=(
            jax.ShapeDtypeStruct((lines, kept, lanes), jnp.float32),
            jax.ShapeDtypeStruct((own, kept), jnp.float32),
        ),
        in_specs=[pl.BlockSpec(memory_space=p) for p in (pl.ANY, pltpu.VMEM, pl.ANY)],
        out_specs=(pl.BlockSpec(memory_space=pl.ANY), pl.BlockSpec(memory_space=pltpu.VMEM)),
        scratch_shapes=[
            pltpu.VMEM((lines, elevs, lanes), jnp.float32),
            pltpu.VMEM((kept, elevs), jnp.float32),
            pltpu.VMEM((elevs, elevs), jnp.float32),
            pltpu.VMEM((lines, kept, lanes), jnp.float32),
            pltpu.VMEM((elevs, kept), jnp.float32),
            pltpu.SemaphoreType.DMA((chunks,)),
            pltpu.SemaphoreType.DMA,
            pltpu.SemaphoreType.DMA((chunks,)),
        ],
        compiler_params=pltpu.CompilerParams(vmem_limit_bytes=48 * 1024 * 1024),
        cost_estimate=pl.CostEstimate(
            flops=6 * lines * lanes * elevs * kept, bytes_accessed=2 * x.size * 4, transcendentals=0
        ),
        name="basis_core",
    )(x, packed, start)


def per_device(frames, start_basis):
    regrouped, packed = gather_gram(frames)
    return basis_core(regrouped, packed, start_basis.T, frames.shape[1])


def solution(mesh):
    return jax.shard_map(
        per_device,
        mesh=mesh,
        in_specs=(P("lat", "elev", None), P()),
        out_specs=(P("lat", None, "elev"), P("elev", None)),
        check_vma=False,
    )
```

```python
import functools

import jax
import jax.numpy as jnp
from jax import lax
from jax.experimental import pallas as pl
from jax.experimental.pallas import tpu as pltpu
from jax.sharding import PartitionSpec as P

ITERS = 3
HIGHEST = lax.Precision.HIGHEST
LANES = 128
STEP = 2
CORE_STEP = 16
Z = 4
X = 4
PARTS = ((0, 24), (24, 16))


def dot_nt(a, b):
    return lax.dot_general(
        a, b, (((1,), (1,)), ((), ())), precision=HIGHEST, preferred_element_type=jnp.float32
    )


def hops(offset):
    return min(offset[0], Z - offset[0]) + min(offset[1], X - offset[1])


def gather_gram_kernel(
    frames, x_out, g_out, buf, gacc, packed, half_in, half, ring_in, part, y_in, total, half_all,
    recv, send, ar_recv, ar_send, out_sem,
):
    lines = frames.shape[0]
    own = frames.shape[1]
    chunks = lines // STEP
    lat = lax.axis_index("lat")
    elev = lax.axis_index("elev")
    core = lax.rem(lat, 2)
    y = lat // 2
    x = lax.rem(elev, X)
    z = elev // X
    partner = lat + 1 - 2 * core
    offsets = sorted([(dz, dx) for dz in range(Z) for dx in range(X) if dz or dx], key=hops)
    far_first = [lax.rem(z + dz, Z) * X + lax.rem(x + dx, X) for dz, dx in reversed(offsets)]
    peers = []
    for n in range(len(far_first)):
        peers.append(far_first[n // 2] if n % 2 else far_first[len(far_first) - 1 - n // 2])
    y_peers = [lax.rem(y + dy, 4) * 2 + core for dy in (2, 1, 3)]

    barrier = pltpu.get_barrier_semaphore()
    for p in peers:
        pl.semaphore_signal(barrier, inc=1, device_id={"elev": p}, device_id_type=pl.DeviceIdType.MESH)
    for q in y_peers + [partner]:
        pl.semaphore_signal(barrier, inc=1, device_id={"lat": q}, device_id_type=pl.DeviceIdType.MESH)
    pl.semaphore_wait(barrier, len(peers) + len(y_peers) + 1)

    gacc[...] = jnp.zeros_like(gacc)
    mine = pl.ds(pl.multiple_of(elev * own, own), own)

    def issue(c, _):
        rows = pl.ds(c * STEP, STEP)
        for p in peers:
            pltpu.make_async_remote_copy(
                src_ref=frames.at[rows, :, pl.ds(pl.multiple_of(p * LANES, LANES), LANES)],
                dst_ref=buf.at[rows, mine, :],
                send_sem=send.at[c],
                recv_sem=recv.at[c],
                device_id={"elev": p},
                device_id_type=pl.DeviceIdType.MESH,
            ).start()
        pltpu.make_async_copy(
            frames.at[rows, :, pl.ds(pl.multiple_of(elev * LANES, LANES), LANES)],
            buf.at[rows, mine, :],
            recv.at[c],
        ).start()
        return 0

    lax.fori_loop(0, chunks, issue, 0)

    def consume(c, _):
        rows = pl.ds(c * STEP, STEP)
        pltpu.make_async_copy(buf.at[rows], buf.at[rows], recv.at[c]).wait()
        pltpu.make_async_copy(buf.at[rows], x_out.at[rows], out_sem.at[c]).start()
        block = jnp.concatenate([buf[c * STEP + i] for i in range(STEP)], axis=1)
        low, high = block[:256], block[256:]
        gacc[0] += dot_nt(low, low)
        gacc[1] += dot_nt(high, low)
        gacc[2] += dot_nt(high, high)
        return 0

    lax.fori_loop(0, chunks, consume, 0)

    places = [(0, 0, 0), (0, 1, 0), (0, 1, 1), (1, 0, 0), (1, 0, 1), (1, 1, 0), (1, 1, 1), (2, 0, 0), (2, 1, 0), (2, 1, 1)]
    blocks = [gacc[g, pl.ds(i * 128, 128), pl.ds(j * 128, 128)] for g, i, j in places]
    packed[...] = jnp.concatenate(blocks, axis=0).reshape(packed.shape)

    plane = Z * X
    parts = [(k, pl.ds(first, count)) for k, (first, count) in enumerate(PARTS)]
    kept = pl.ds(core * plane, plane)
    given = pl.ds((1 - core) * plane, plane)

    def to_partner(src, dst, hop, k):
        return pltpu.make_async_remote_copy(
            src_ref=src,
            dst_ref=dst,
            send_sem=ar_send.at[hop, k],
            recv_sem=ar_recv.at[hop, k],
            device_id={"lat": partner},
            device_id_type=pl.DeviceIdType.MESH,
        )

    def send_all(src_of, dst, axis, targets, hop, k, mine_src):
        for p in targets:
            pltpu.make_async_remote_copy(
                src_ref=src_of(p),
                dst_ref=dst,
                send_sem=ar_send.at[hop, k],
                recv_sem=ar_recv.at[hop, k],
                device_id={axis: p},
                device_id_type=pl.DeviceIdType.MESH,
            ).start()
        pltpu.make_async_copy(mine_src, dst, ar_recv.at[hop, k]).start()

    swaps = [to_partner(packed.at[given, rows], half_in.at[:, rows], 0, k) for k, rows in parts]
    for swap in swaps:
        swap.start()
    for k, rows in parts:
        swaps[k].wait()
        half[:, rows] = packed[kept, rows] + half_in[:, rows]
        send_all(lambda p: half.at[p, rows], ring_in.at[elev, rows], "elev", far_first, 1, k, half.at[elev, rows])
    for k, rows in parts:
        pltpu.make_async_copy(ring_in.at[:, rows], ring_in.at[:, rows], ar_recv.at[1, k]).wait()
        part[rows] = jnp.sum(ring_in[:, rows], axis=0)
        send_all(lambda q: part.at[rows], y_in.at[y, rows], "lat", y_peers, 2, k, part.at[rows])
    for k, rows in parts:
        pltpu.make_async_copy(y_in.at[:, rows], y_in.at[:, rows], ar_recv.at[2, k]).wait()
        total[rows] = (y_in[0, rows] + y_in[1, rows]) + (y_in[2, rows] + y_in[3, rows])
        send_all(lambda p: total.at[rows], half_all.at[elev, rows], "elev", far_first, 3, k, total.at[rows])
    swaps = [to_partner(half_all.at[:, rows], g_out.at[kept, rows], 4, k) for k, rows in parts]
    for k, rows in parts:
        pltpu.make_async_copy(half_all.at[:, rows], half_all.at[:, rows], ar_recv.at[3, k]).wait()
        swaps[k].start()
        g_out[kept, rows] = half_all[:, rows]
    for swap in swaps:
        swap.wait()

    n = plane - 1
    for k, rows in parts:
        for hop, gone in ((1, half.at[pl.ds(0, n), rows]), (2, y_in.at[pl.ds(0, 3), rows]), (3, half.at[pl.ds(0, n), rows])):
            pltpu.make_async_copy(gone, gone, ar_send.at[hop, k]).wait()

    def drain(c, _):
        rows = pl.ds(c * STEP, STEP)
        gone = buf.at[rows, pl.ds(0, n * own), :]
        pltpu.make_async_copy(gone, gone, send.at[c]).wait()
        pltpu.make_async_copy(buf.at[rows], x_out.at[rows], out_sem.at[c]).wait()
        return 0

    lax.fori_loop(0, chunks, drain, 0)


def gather_gram(frames):
    lines, own, columns = frames.shape
    elevs = own * Z * X
    chunks = lines // STEP
    plane = Z * X
    shard = 1280 // (2 * plane)
    return pl.pallas_call(
        gather_gram_kernel,
        out_shape=(
            jax.ShapeDtypeStruct((lines, elevs, LANES), jnp.float32),
            jax.ShapeDtypeStruct((2 * plane, shard, LANES), jnp.float32),
        ),
        in_specs=[pl.BlockSpec(memory_space=pl.ANY)],
        out_specs=(pl.BlockSpec(memory_space=pl.ANY), pl.BlockSpec(memory_space=pltpu.VMEM)),
        scratch_shapes=[
            pltpu.VMEM((lines, elevs, LANES), jnp.float32),
            pltpu.VMEM((3, 256, 256), jnp.float32),
            pltpu.VMEM((2 * plane, shard, LANES), jnp.float32),
            pltpu.VMEM((plane, shard, LANES), jnp.float32),
            pltpu.VMEM((plane, shard, LANES), jnp.float32),
            pltpu.VMEM((plane, shard, LANES), jnp.float32),
            pltpu.VMEM((shard, LANES), jnp.float32),
            pltpu.VMEM((4, shard, LANES), jnp.float32),
            pltpu.VMEM((shard, LANES), jnp.float32),
            pltpu.VMEM((plane, shard, LANES), jnp.float32),
            pltpu.SemaphoreType.DMA((chunks,)),
            pltpu.SemaphoreType.DMA((chunks,)),
            pltpu.SemaphoreType.DMA((5, len(PARTS))),
            pltpu.SemaphoreType.DMA((5, len(PARTS))),
            pltpu.SemaphoreType.DMA((chunks,)),
        ],
        compiler_params=pltpu.CompilerParams(
            collective_id=0, has_side_effects=True, vmem_limit_bytes=48 * 1024 * 1024
        ),
        cost_estimate=pl.CostEstimate(
            flops=2 * lines * LANES * elevs * elevs, bytes_accessed=3 * frames.size * 4, transcendentals=0
        ),
        name="gather_gram",
    )(frames)


def iota(shape, dim):
    return lax.broadcasted_iota(jnp.int32, shape, dim)


def dot_nn(a, b):
    return jnp.dot(a, b, precision=HIGHEST, preferred_element_type=jnp.float32)


def split(v):
    high = v.astype(jnp.bfloat16)
    return high, (v - high.astype(jnp.float32)).astype(jnp.bfloat16)


def cholesky_inverse(m):
    n = m.shape[0]
    tiles = n // 8
    sub, lane = iota((8, n), 0), iota((8, n), 1)

    def up(row):
        return jnp.broadcast_to(row, (8, n))

    def along(tile, j):
        return jnp.broadcast_to(tile[:, j : j + 1], (8, n))

    a = [m[8 * i : 8 * i + 8, :] for i in range(tiles)]
    out = []
    diagonal = [along(a[0], t) for t in range(8)]
    for p in range(tiles):
        j = 8 * p
        columns = [[along(a[i], j + t) for i in range(p + 1, tiles)] for t in range(8)]
        ahead = [along(a[p + 1], j + 8 + s) for s in range(8)] if p + 1 < tiles else []
        panel = (lane >= j) & (lane < j + 8)
        row = jnp.where(panel, jnp.where(lane == sub + j, 1.0, 0.0), a[p])
        below = [jnp.where(panel, 0.0, a[i]) for i in range(p + 1, tiles)]
        pivots = diagonal[0]
        for t in range(8):
            pivot = up(diagonal[t][t : t + 1, :])
            inverse = 1.0 / pivot
            if t:
                pivots = jnp.where(sub == t, pivot, pivots)
            g = jnp.where(sub > t, diagonal[t] * inverse, 0.0)
            f = [q * inverse for q in columns[t]]
            for s in range(t + 1, 8):
                scale = up(diagonal[t][s : s + 1, :])
                diagonal[s] = diagonal[s] - g * scale
                columns[s] = [q - h * scale for q, h in zip(columns[s], f)]
            ahead = [q - f[0] * up(columns[t][0][s : s + 1, :]) for s, q in enumerate(ahead)]
            pivot_row = up(row[t : t + 1, :])
            row = row - g * pivot_row
            below = [q - h * pivot_row for q, h in zip(below, f)]
        a = a[: p + 1] + below
        diagonal = ahead
        out.append(jnp.where(lane < j + 8, row, 0.0) * lax.rsqrt(pivots))
    return jnp.concatenate(out, axis=0)


def orth_again(w, result):
    m = dot_nt(w, w)
    row, column = iota(m.shape, 0), iota(m.shape, 1)
    e = m - jnp.where(row == column, 1.0, 0.0)
    lower = jnp.where(row > column, e, jnp.where(row == column, 0.5 * e, 0.0))
    result[...] = w - jnp.dot(lower.astype(jnp.bfloat16), w.astype(jnp.bfloat16), preferred_element_type=jnp.float32)

    @pl.when(jnp.logical_not(jnp.sum(e * e) <= 3e-8))
    def _():
        result[...] = dot_nn(cholesky_inverse(m), w)


def basis_core_kernel(x, packed, start, core, basis_out, buf, first, gram, out, turned, in_sem, start_sem, out_sem):
    chunks = x.shape[0] // CORE_STEP

    def load(c):
        rows = pl.ds(c * CORE_STEP, CORE_STEP)
        return pltpu.make_async_copy(x.at[rows], buf.at[rows], in_sem.at[c])

    def store(c):
        rows = pl.ds(c * CORE_STEP, CORE_STEP)
        return pltpu.make_async_copy(out.at[rows], core.at[rows], out_sem.at[c])

    begin = pltpu.make_async_copy(start, first, start_sem)
    begin.start()
    for c in range(chunks):
        load(c).start()

    places = [(0, 0), (1, 0), (1, 1), (2, 0), (2, 1), (3, 0), (3, 1), (2, 2), (3, 2), (3, 3)]
    for n, (i, j) in enumerate(places):
        tile = packed[pl.ds(n * 128, 128), :]
        gram[pl.ds(i * 128, 128), pl.ds(j * 128, 128)] = tile
        if i != j:
            gram[pl.ds(j * 128, 128), pl.ds(i * 128, 128)] = tile.T

    def turn(_, carry):
        w = dot_nn(first[...], gram[...])
        w = dot_nn(cholesky_inverse(dot_nt(w, w)), w)
        orth_again(w, first)
        return carry

    begin.wait()
    lax.fori_loop(0, ITERS, turn, 0)
    basis = first[...]
    turned[...] = basis.T
    own = basis_out.shape[0]
    basis_out[...] = turned[pl.ds(pl.multiple_of(lax.axis_index("elev") * own, 8), own), :]

    high, low = split(basis)
    both = jnp.concatenate([high, low], axis=0)
    kept = basis.shape[0]

    for c in range(chunks):
        load(c).wait()

    def project(c, _):
        for i in range(0, CORE_STEP, 2):
            l = c * CORE_STEP + i
            xh, xl = split(jnp.concatenate([buf[l], buf[l + 1]], axis=1))
            r = jnp.dot(both, xh, preferred_element_type=jnp.float32)
            q = jnp.dot(high, xl, preferred_element_type=jnp.float32)
            s = r[:kept] + (r[kept:] + q)
            out[l] = s[:, :LANES]
            out[l + 1] = s[:, LANES:]
        store(c).start()
        return 0

    lax.fori_loop(0, chunks, project, 0)

    def drain(c, _):
        store(c).wait()
        return 0

    lax.fori_loop(0, chunks, drain, 0)


def basis_core(x, packed, start, own):
    lines, elevs, lanes = x.shape
    kept = start.shape[0]
    chunks = lines // CORE_STEP
    return pl.pallas_call(
        basis_core_kernel,
        out_shape=(
            jax.ShapeDtypeStruct((lines, kept, lanes), jnp.float32),
            jax.ShapeDtypeStruct((own, kept), jnp.float32),
        ),
        in_specs=[pl.BlockSpec(memory_space=p) for p in (pl.ANY, pltpu.VMEM, pl.ANY)],
        out_specs=(pl.BlockSpec(memory_space=pl.ANY), pl.BlockSpec(memory_space=pltpu.VMEM)),
        scratch_shapes=[
            pltpu.VMEM((lines, elevs, lanes), jnp.float32),
            pltpu.VMEM((kept, elevs), jnp.float32),
            pltpu.VMEM((elevs, elevs), jnp.float32),
            pltpu.VMEM((lines, kept, lanes), jnp.float32),
            pltpu.VMEM((elevs, kept), jnp.float32),
            pltpu.SemaphoreType.DMA((chunks,)),
            pltpu.SemaphoreType.DMA,
            pltpu.SemaphoreType.DMA((chunks,)),
        ],
        compiler_params=pltpu.CompilerParams(vmem_limit_bytes=48 * 1024 * 1024),
        cost_estimate=pl.CostEstimate(
            flops=6 * lines * lanes * elevs * kept, bytes_accessed=2 * x.size * 4, transcendentals=0
        ),
        name="basis_core",
    )(x, packed, start)


def per_device(frames, start_basis):
    regrouped, packed = gather_gram(frames)
    return basis_core(regrouped, packed.reshape(-1, LANES), start_basis.T, frames.shape[1])


def solution(mesh):
    return jax.shard_map(
        per_device,
        mesh=mesh,
        in_specs=(P("lat", "elev", None), P()),
        out_specs=(P("lat", None, "elev"), P("elev", None)),
        check_vma=False,
    )
```

```python
import functools

import jax
import jax.numpy as jnp
from jax import lax
from jax.experimental import pallas as pl
from jax.experimental.pallas import tpu as pltpu
from jax.sharding import PartitionSpec as P

ITERS = 3
HIGHEST = lax.Precision.HIGHEST
LANES = 128
STEP = 4
CORE_STEP = 16
Z = 4
X = 4
PARTS = ((0, 24), (24, 16))


def dot_nt(a, b):
    return lax.dot_general(
        a, b, (((1,), (1,)), ((), ())), precision=HIGHEST, preferred_element_type=jnp.float32
    )


def hops(offset):
    return min(offset[0], Z - offset[0]) + min(offset[1], X - offset[1])


def gather_gram_kernel(
    frames, x_out, g_out, buf, gacc, packed, half_in, half, ring_in, part, y_in, total, half_all,
    recv, send, ar_recv, ar_send, out_sem,
):
    lines = frames.shape[0]
    own = frames.shape[1]
    chunks = lines // STEP
    lat = lax.axis_index("lat")
    elev = lax.axis_index("elev")
    core = lax.rem(lat, 2)
    y = lat // 2
    x = lax.rem(elev, X)
    z = elev // X
    partner = lat + 1 - 2 * core
    offsets = sorted([(dz, dx) for dz in range(Z) for dx in range(X) if dz or dx], key=hops)
    far_first = [lax.rem(z + dz, Z) * X + lax.rem(x + dx, X) for dz, dx in reversed(offsets)]
    peers = []
    for n in range(len(far_first)):
        peers.append(far_first[n // 2] if n % 2 else far_first[len(far_first) - 1 - n // 2])
    y_peers = [lax.rem(y + dy, 4) * 2 + core for dy in (2, 1, 3)]

    barrier = pltpu.get_barrier_semaphore()
    for p in peers:
        pl.semaphore_signal(barrier, inc=1, device_id={"elev": p}, device_id_type=pl.DeviceIdType.MESH)
    for q in y_peers + [partner]:
        pl.semaphore_signal(barrier, inc=1, device_id={"lat": q}, device_id_type=pl.DeviceIdType.MESH)
    pl.semaphore_wait(barrier, len(peers) + len(y_peers) + 1)

    gacc[...] = jnp.zeros_like(gacc)
    mine = pl.ds(pl.multiple_of(elev * own, own), own)

    def issue(c, _):
        rows = pl.ds(c * STEP, STEP)
        for p in peers:
            pltpu.make_async_remote_copy(
                src_ref=frames.at[rows, :, pl.ds(pl.multiple_of(p * LANES, LANES), LANES)],
                dst_ref=buf.at[rows, mine, :],
                send_sem=send.at[c],
                recv_sem=recv.at[c],
                device_id={"elev": p},
                device_id_type=pl.DeviceIdType.MESH,
            ).start()
        pltpu.make_async_copy(
            frames.at[rows, :, pl.ds(pl.multiple_of(elev * LANES, LANES), LANES)],
            buf.at[rows, mine, :],
            recv.at[c],
        ).start()
        return 0

    lax.fori_loop(0, chunks, issue, 0)

    def consume(c, _):
        rows = pl.ds(c * STEP, STEP)
        pltpu.make_async_copy(buf.at[rows], buf.at[rows], recv.at[c]).wait()
        pltpu.make_async_copy(buf.at[rows], x_out.at[rows], out_sem.at[c]).start()
        block = jnp.concatenate([buf[c * STEP + i] for i in range(STEP)], axis=1)
        low, high = block[:256], block[256:]
        gacc[0] += dot_nt(low, low)
        gacc[1] += dot_nt(high, low)
        gacc[2] += dot_nt(high, high)
        return 0

    lax.fori_loop(0, chunks, consume, 0)

    places = [(0, 0, 0), (0, 1, 0), (0, 1, 1), (1, 0, 0), (1, 0, 1), (1, 1, 0), (1, 1, 1), (2, 0, 0), (2, 1, 0), (2, 1, 1)]
    blocks = [gacc[g, pl.ds(i * 128, 128), pl.ds(j * 128, 128)] for g, i, j in places]
    packed[...] = jnp.concatenate(blocks, axis=0).reshape(packed.shape)

    plane = Z * X
    parts = [(k, pl.ds(first, count)) for k, (first, count) in enumerate(PARTS)]
    kept = pl.ds(core * plane, plane)
    given = pl.ds((1 - core) * plane, plane)

    def to_partner(src, dst, hop, k):
        return pltpu.make_async_remote_copy(
            src_ref=src,
            dst_ref=dst,
            send_sem=ar_send.at[hop, k],
            recv_sem=ar_recv.at[hop, k],
            device_id={"lat": partner},
            device_id_type=pl.DeviceIdType.MESH,
        )

    def send_all(src_of, dst, axis, targets, hop, k, mine_src):
        for p in targets:
            pltpu.make_async_remote_copy(
                src_ref=src_of(p),
                dst_ref=dst,
                send_sem=ar_send.at[hop, k],
                recv_sem=ar_recv.at[hop, k],
                device_id={axis: p},
                device_id_type=pl.DeviceIdType.MESH,
            ).start()
        pltpu.make_async_copy(mine_src, dst, ar_recv.at[hop, k]).start()

    swaps = [to_partner(packed.at[given, rows], half_in.at[:, rows], 0, k) for k, rows in parts]
    for swap in swaps:
        swap.start()
    for k, rows in parts:
        swaps[k].wait()
        half[:, rows] = packed[kept, rows] + half_in[:, rows]
        send_all(lambda p: half.at[p, rows], ring_in.at[elev, rows], "elev", far_first, 1, k, half.at[elev, rows])
    def drain(c, _):
        rows = pl.ds(c * STEP, STEP)
        gone = buf.at[rows, pl.ds(0, (plane - 1) * own), :]
        pltpu.make_async_copy(gone, gone, send.at[c]).wait()
        pltpu.make_async_copy(buf.at[rows], x_out.at[rows], out_sem.at[c]).wait()
        return 0

    lax.fori_loop(0, chunks, drain, 0)

    for k, rows in parts:
        pltpu.make_async_copy(ring_in.at[:, rows], ring_in.at[:, rows], ar_recv.at[1, k]).wait()
        part[rows] = jnp.sum(ring_in[:, rows], axis=0)
        send_all(lambda q: part.at[rows], y_in.at[y, rows], "lat", y_peers, 2, k, part.at[rows])
    for k, rows in parts:
        pltpu.make_async_copy(y_in.at[:, rows], y_in.at[:, rows], ar_recv.at[2, k]).wait()
        total[rows] = (y_in[0, rows] + y_in[1, rows]) + (y_in[2, rows] + y_in[3, rows])
        send_all(lambda p: total.at[rows], half_all.at[elev, rows], "elev", far_first, 3, k, total.at[rows])
    swaps = [to_partner(half_all.at[:, rows], g_out.at[kept, rows], 4, k) for k, rows in parts]
    for k, rows in parts:
        pltpu.make_async_copy(half_all.at[:, rows], half_all.at[:, rows], ar_recv.at[3, k]).wait()
        swaps[k].start()
        g_out[kept, rows] = half_all[:, rows]
    for swap in swaps:
        swap.wait()

    n = plane - 1
    for k, rows in parts:
        for hop, gone in ((1, half.at[pl.ds(0, n), rows]), (2, y_in.at[pl.ds(0, 3), rows]), (3, half.at[pl.ds(0, n), rows])):
            pltpu.make_async_copy(gone, gone, ar_send.at[hop, k]).wait()


def gather_gram(frames):
    lines, own, columns = frames.shape
    elevs = own * Z * X
    chunks = lines // STEP
    plane = Z * X
    shard = 1280 // (2 * plane)
    return pl.pallas_call(
        gather_gram_kernel,
        out_shape=(
            jax.ShapeDtypeStruct((lines, elevs, LANES), jnp.float32),
            jax.ShapeDtypeStruct((2 * plane, shard, LANES), jnp.float32),
        ),
        in_specs=[pl.BlockSpec(memory_space=pl.ANY)],
        out_specs=(pl.BlockSpec(memory_space=pl.ANY), pl.BlockSpec(memory_space=pltpu.VMEM)),
        scratch_shapes=[
            pltpu.VMEM((lines, elevs, LANES), jnp.float32),
            pltpu.VMEM((3, 256, 256), jnp.float32),
            pltpu.VMEM((2 * plane, shard, LANES), jnp.float32),
            pltpu.VMEM((plane, shard, LANES), jnp.float32),
            pltpu.VMEM((plane, shard, LANES), jnp.float32),
            pltpu.VMEM((plane, shard, LANES), jnp.float32),
            pltpu.VMEM((shard, LANES), jnp.float32),
            pltpu.VMEM((4, shard, LANES), jnp.float32),
            pltpu.VMEM((shard, LANES), jnp.float32),
            pltpu.VMEM((plane, shard, LANES), jnp.float32),
            pltpu.SemaphoreType.DMA((chunks,)),
            pltpu.SemaphoreType.DMA((chunks,)),
            pltpu.SemaphoreType.DMA((5, len(PARTS))),
            pltpu.SemaphoreType.DMA((5, len(PARTS))),
            pltpu.SemaphoreType.DMA((chunks,)),
        ],
        compiler_params=pltpu.CompilerParams(
            collective_id=0, has_side_effects=True, vmem_limit_bytes=48 * 1024 * 1024
        ),
        cost_estimate=pl.CostEstimate(
            flops=2 * lines * LANES * elevs * elevs, bytes_accessed=3 * frames.size * 4, transcendentals=0
        ),
        name="gather_gram",
    )(frames)


def iota(shape, dim):
    return lax.broadcasted_iota(jnp.int32, shape, dim)


def dot_nn(a, b):
    return jnp.dot(a, b, precision=HIGHEST, preferred_element_type=jnp.float32)


def split(v):
    high = v.astype(jnp.bfloat16)
    return high, (v - high.astype(jnp.float32)).astype(jnp.bfloat16)


def cholesky_inverse(m):
    n = m.shape[0]
    tiles = n // 8
    sub, lane = iota((8, n), 0), iota((8, n), 1)

    def up(row):
        return jnp.broadcast_to(row, (8, n))

    def along(tile, j):
        return jnp.broadcast_to(tile[:, j : j + 1], (8, n))

    a = [m[8 * i : 8 * i + 8, :] for i in range(tiles)]
    out = []
    diagonal = [along(a[0], t) for t in range(8)]
    for p in range(tiles):
        j = 8 * p
        columns = [[along(a[i], j + t) for i in range(p + 1, tiles)] for t in range(8)]
        ahead = [along(a[p + 1], j + 8 + s) for s in range(8)] if p + 1 < tiles else []
        panel = (lane >= j) & (lane < j + 8)
        row = jnp.where(panel, jnp.where(lane == sub + j, 1.0, 0.0), a[p])
        below = [jnp.where(panel, 0.0, a[i]) for i in range(p + 1, tiles)]
        pivots = diagonal[0]
        for t in range(8):
            pivot = up(diagonal[t][t : t + 1, :])
            inverse = 1.0 / pivot
            if t:
                pivots = jnp.where(sub == t, pivot, pivots)
            g = jnp.where(sub > t, diagonal[t] * inverse, 0.0)
            f = [q * inverse for q in columns[t]]
            for s in range(t + 1, 8):
                scale = up(diagonal[t][s : s + 1, :])
                diagonal[s] = diagonal[s] - g * scale
                columns[s] = [q - h * scale for q, h in zip(columns[s], f)]
            ahead = [q - f[0] * up(columns[t][0][s : s + 1, :]) for s, q in enumerate(ahead)]
            pivot_row = up(row[t : t + 1, :])
            row = row - g * pivot_row
            below = [q - h * pivot_row for q, h in zip(below, f)]
        a = a[: p + 1] + below
        diagonal = ahead
        out.append(jnp.where(lane < j + 8, row, 0.0) * lax.rsqrt(pivots))
    return jnp.concatenate(out, axis=0)


def split3(v):
    high = v.astype(jnp.bfloat16)
    rest = v - high.astype(jnp.float32)
    middle = rest.astype(jnp.bfloat16)
    return high, middle, (rest - middle.astype(jnp.float32)).astype(jnp.bfloat16)


def dot_parts(a, b):
    rows = a.shape[0]
    a = split3(a)
    first = jnp.dot(jnp.concatenate(a, axis=0), b[0][...], preferred_element_type=jnp.float32)
    second = jnp.dot(jnp.concatenate(a[:2], axis=0), b[1][...], preferred_element_type=jnp.float32)
    third = jnp.dot(a[0], b[2][...], preferred_element_type=jnp.float32)
    return first[:rows] + (first[rows : 2 * rows] + second[:rows] + (first[2 * rows :] + second[rows:] + third))


def near_identity(m):
    row, column = iota(m.shape, 0), iota(m.shape, 1)
    e = m - jnp.where(row == column, 1.0, 0.0)
    lower = jnp.where(row > column, e, jnp.where(row == column, 0.5 * e, 0.0))
    return jnp.sum(e * e) <= 3e-8, lower.astype(jnp.bfloat16)


def basis_core_kernel(x, packed, start, core, basis_out, buf, first, gram, out, turned, wide, gh, gm, gl, in_sem, start_sem, out_sem):
    chunks = x.shape[0] // CORE_STEP

    def load(c):
        rows = pl.ds(c * CORE_STEP, CORE_STEP)
        return pltpu.make_async_copy(x.at[rows], buf.at[rows], in_sem.at[c])

    def store(c):
        rows = pl.ds(c * CORE_STEP, CORE_STEP)
        return pltpu.make_async_copy(out.at[rows], core.at[rows], out_sem.at[c])

    begin = pltpu.make_async_copy(start, first, start_sem)
    begin.start()
    for c in range(chunks):
        load(c).start()

    places = [(0, 0), (1, 0), (1, 1), (2, 0), (2, 1), (3, 0), (3, 1), (2, 2), (3, 2), (3, 3)]
    for n, (i, j) in enumerate(places):
        tile = packed[pl.ds(n * 128, 128), :]
        gram[pl.ds(i * 128, 128), pl.ds(j * 128, 128)] = tile
        if i != j:
            gram[pl.ds(j * 128, 128), pl.ds(i * 128, 128)] = tile.T

    for part, value in zip((gh, gm, gl), split3(gram[...])):
        part[...] = value

    begin.wait()
    wide[...] = dot_parts(first[...], (gh, gm, gl))

    def turn(last):
        w = wide[...]
        w = dot_nn(cholesky_inverse(dot_nt(w, w)), w)
        m = dot_nt(w, w)
        near, lower = near_identity(m)

        def corrected(v):
            return v - jnp.dot(lower, v.astype(jnp.bfloat16), preferred_element_type=jnp.float32)

        if last:
            first[...] = corrected(w)
        else:
            wide[...] = corrected(dot_parts(w, (gh, gm, gl)))

        @pl.when(jnp.logical_not(near))
        def _():
            first[...] = dot_nn(cholesky_inverse(m), w)
            if not last:
                wide[...] = dot_parts(first[...], (gh, gm, gl))

    def earlier_turn(_, carry):
        turn(False)
        return carry

    lax.fori_loop(0, ITERS - 1, earlier_turn, 0)
    turn(True)
    basis = first[...]
    turned[...] = basis.T
    own = basis_out.shape[0]
    basis_out[...] = turned[pl.ds(pl.multiple_of(lax.axis_index("elev") * own, 8), own), :]

    high, low = split(basis)
    both = jnp.concatenate([high, low], axis=0)
    kept = basis.shape[0]

    for c in range(chunks):
        load(c).wait()

    def project(c, _):
        for i in range(0, CORE_STEP, 2):
            l = c * CORE_STEP + i
            xh, xl = split(jnp.concatenate([buf[l], buf[l + 1]], axis=1))
            r = jnp.dot(both, xh, preferred_element_type=jnp.float32)
            q = jnp.dot(high, xl, preferred_element_type=jnp.float32)
            s = r[:kept] + (r[kept:] + q)
            out[l] = s[:, :LANES]
            out[l + 1] = s[:, LANES:]
        store(c).start()
        return 0

    lax.fori_loop(0, chunks, project, 0)

    def drain(c, _):
        store(c).wait()
        return 0

    lax.fori_loop(0, chunks, drain, 0)


def basis_core(x, packed, start, own):
    lines, elevs, lanes = x.shape
    kept = start.shape[0]
    chunks = lines // CORE_STEP
    return pl.pallas_call(
        basis_core_kernel,
        out_shape=(
            jax.ShapeDtypeStruct((lines, kept, lanes), jnp.float32),
            jax.ShapeDtypeStruct((own, kept), jnp.float32),
        ),
        in_specs=[pl.BlockSpec(memory_space=p) for p in (pl.ANY, pltpu.VMEM, pl.ANY)],
        out_specs=(pl.BlockSpec(memory_space=pl.ANY), pl.BlockSpec(memory_space=pltpu.VMEM)),
        scratch_shapes=[
            pltpu.VMEM((lines, elevs, lanes), jnp.float32),
            pltpu.VMEM((kept, elevs), jnp.float32),
            pltpu.VMEM((elevs, elevs), jnp.float32),
            pltpu.VMEM((lines, kept, lanes), jnp.float32),
            pltpu.VMEM((elevs, kept), jnp.float32),
            pltpu.VMEM((kept, elevs), jnp.float32),
            pltpu.VMEM((elevs, elevs), jnp.bfloat16),
            pltpu.VMEM((elevs, elevs), jnp.bfloat16),
            pltpu.VMEM((elevs, elevs), jnp.bfloat16),
            pltpu.SemaphoreType.DMA((chunks,)),
            pltpu.SemaphoreType.DMA,
            pltpu.SemaphoreType.DMA((chunks,)),
        ],
        compiler_params=pltpu.CompilerParams(vmem_limit_bytes=48 * 1024 * 1024),
        cost_estimate=pl.CostEstimate(
            flops=6 * lines * lanes * elevs * kept, bytes_accessed=2 * x.size * 4, transcendentals=0
        ),
        name="basis_core",
    )(x, packed, start)


def per_device(frames, start_basis):
    regrouped, packed = gather_gram(frames)
    return basis_core(regrouped, packed.reshape(-1, LANES), start_basis.T, frames.shape[1])


def solution(mesh):
    return jax.shard_map(
        per_device,
        mesh=mesh,
        in_specs=(P("lat", "elev", None), P()),
        out_specs=(P("lat", None, "elev"), P("elev", None)),
        check_vma=False,
    )
```

```python
import functools

import jax
import jax.numpy as jnp
from jax import lax
from jax.experimental import pallas as pl
from jax.experimental.pallas import tpu as pltpu
from jax.sharding import PartitionSpec as P

ITERS = 3
HIGHEST = lax.Precision.HIGHEST
LANES = 128
STEP = 4
LAST = (2, 1, 1)
CORE_STEP = 16
Z = 4
X = 4
PARTS = ((0, 24), (24, 16))


def dot_nt(a, b):
    return lax.dot_general(
        a, b, (((1,), (1,)), ((), ())), precision=HIGHEST, preferred_element_type=jnp.float32
    )


def hops(offset):
    return min(offset[0], Z - offset[0]) + min(offset[1], X - offset[1])


def gather_gram_kernel(
    frames, x_out, g_out, buf, gacc, packed, half_in, half, ring_in, part, y_in, total, half_all,
    recv, send, ar_recv, ar_send, out_sem,
):
    lines = frames.shape[0]
    own = frames.shape[1]
    chunks = (lines - sum(LAST)) // STEP
    tail = [(chunks + n, lines - sum(LAST[n:]), count) for n, count in enumerate(LAST)]
    lat = lax.axis_index("lat")
    elev = lax.axis_index("elev")
    core = lax.rem(lat, 2)
    y = lat // 2
    x = lax.rem(elev, X)
    z = elev // X
    partner = lat + 1 - 2 * core
    offsets = sorted([(dz, dx) for dz in range(Z) for dx in range(X) if dz or dx], key=hops)
    far_first = [lax.rem(z + dz, Z) * X + lax.rem(x + dx, X) for dz, dx in reversed(offsets)]
    peers = []
    for n in range(len(far_first)):
        peers.append(far_first[n // 2] if n % 2 else far_first[len(far_first) - 1 - n // 2])
    y_peers = [lax.rem(y + dy, 4) * 2 + core for dy in (2, 1, 3)]

    barrier = pltpu.get_barrier_semaphore()
    for p in peers:
        pl.semaphore_signal(barrier, inc=1, device_id={"elev": p}, device_id_type=pl.DeviceIdType.MESH)
    for q in y_peers + [partner]:
        pl.semaphore_signal(barrier, inc=1, device_id={"lat": q}, device_id_type=pl.DeviceIdType.MESH)
    pl.semaphore_wait(barrier, len(peers) + len(y_peers) + 1)

    gacc[...] = jnp.zeros_like(gacc)
    mine = pl.ds(pl.multiple_of(elev * own, own), own)

    def issue(c, first, count):
        rows = pl.ds(first, count)
        for p in peers:
            pltpu.make_async_remote_copy(
                src_ref=frames.at[rows, :, pl.ds(pl.multiple_of(p * LANES, LANES), LANES)],
                dst_ref=buf.at[rows, mine, :],
                send_sem=send.at[c],
                recv_sem=recv.at[c],
                device_id={"elev": p},
                device_id_type=pl.DeviceIdType.MESH,
            ).start()
        pltpu.make_async_copy(
            frames.at[rows, :, pl.ds(pl.multiple_of(elev * LANES, LANES), LANES)],
            buf.at[rows, mine, :],
            recv.at[c],
        ).start()
        return 0

    lax.fori_loop(0, chunks, lambda c, _: issue(c, c * STEP, STEP), 0)
    for c, first, count in tail:
        issue(c, first, count)

    def consume(c, first, count):
        rows = pl.ds(first, count)
        pltpu.make_async_copy(buf.at[rows], buf.at[rows], recv.at[c]).wait()
        pltpu.make_async_copy(buf.at[rows], x_out.at[rows], out_sem.at[c]).start()
        block = jnp.concatenate([buf[first + i] for i in range(count)], axis=1)
        low, high = block[:256], block[256:]
        gacc[0] += dot_nt(low, low)
        gacc[1] += dot_nt(high, low)
        gacc[2] += dot_nt(high, high)
        return 0

    lax.fori_loop(0, chunks, lambda c, _: consume(c, c * STEP, STEP), 0)
    for c, first, count in tail:
        consume(c, first, count)

    places = [(0, 0, 0), (0, 1, 0), (0, 1, 1), (1, 0, 0), (1, 0, 1), (1, 1, 0), (1, 1, 1), (2, 0, 0), (2, 1, 0), (2, 1, 1)]
    blocks = [gacc[g, pl.ds(i * 128, 128), pl.ds(j * 128, 128)] for g, i, j in places]
    packed[...] = jnp.concatenate(blocks, axis=0).reshape(packed.shape)

    plane = Z * X
    parts = [(k, pl.ds(first, count)) for k, (first, count) in enumerate(PARTS)]
    kept = pl.ds(core * plane, plane)
    given = pl.ds((1 - core) * plane, plane)

    def to_partner(src, dst, hop, k):
        return pltpu.make_async_remote_copy(
            src_ref=src,
            dst_ref=dst,
            send_sem=ar_send.at[hop, k],
            recv_sem=ar_recv.at[hop, k],
            device_id={"lat": partner},
            device_id_type=pl.DeviceIdType.MESH,
        )

    def send_all(src_of, dst, axis, targets, hop, k, mine_src):
        for p in targets:
            pltpu.make_async_remote_copy(
                src_ref=src_of(p),
                dst_ref=dst,
                send_sem=ar_send.at[hop, k],
                recv_sem=ar_recv.at[hop, k],
                device_id={axis: p},
                device_id_type=pl.DeviceIdType.MESH,
            ).start()
        pltpu.make_async_copy(mine_src, dst, ar_recv.at[hop, k]).start()

    swaps = [to_partner(packed.at[given, rows], half_in.at[:, rows], 0, k) for k, rows in parts]
    for swap in swaps:
        swap.start()
    for k, rows in parts:
        swaps[k].wait()
        half[:, rows] = packed[kept, rows] + half_in[:, rows]
        send_all(lambda p: half.at[p, rows], ring_in.at[elev, rows], "elev", far_first, 1, k, half.at[elev, rows])
    def drain(c, first, count):
        rows = pl.ds(first, count)
        gone = buf.at[rows, pl.ds(0, (plane - 1) * own), :]
        pltpu.make_async_copy(gone, gone, send.at[c]).wait()
        pltpu.make_async_copy(buf.at[rows], x_out.at[rows], out_sem.at[c]).wait()
        return 0

    lax.fori_loop(0, chunks, lambda c, _: drain(c, c * STEP, STEP), 0)
    for c, first, count in tail:
        drain(c, first, count)

    for k, rows in parts:
        pltpu.make_async_copy(ring_in.at[:, rows], ring_in.at[:, rows], ar_recv.at[1, k]).wait()
        part[rows] = jnp.sum(ring_in[:, rows], axis=0)
        send_all(lambda q: part.at[rows], y_in.at[y, rows], "lat", y_peers, 2, k, part.at[rows])
    for k, rows in parts:
        pltpu.make_async_copy(y_in.at[:, rows], y_in.at[:, rows], ar_recv.at[2, k]).wait()
        total[rows] = (y_in[0, rows] + y_in[1, rows]) + (y_in[2, rows] + y_in[3, rows])
        send_all(lambda p: total.at[rows], half_all.at[elev, rows], "elev", far_first, 3, k, total.at[rows])
    swaps = [to_partner(half_all.at[:, rows], g_out.at[kept, rows], 4, k) for k, rows in parts]
    for k, rows in parts:
        pltpu.make_async_copy(half_all.at[:, rows], half_all.at[:, rows], ar_recv.at[3, k]).wait()
        swaps[k].start()
        g_out[kept, rows] = half_all[:, rows]
    for swap in swaps:
        swap.wait()

    n = plane - 1
    for k, rows in parts:
        for hop, gone in ((1, half.at[pl.ds(0, n), rows]), (2, y_in.at[pl.ds(0, 3), rows]), (3, half.at[pl.ds(0, n), rows])):
            pltpu.make_async_copy(gone, gone, ar_send.at[hop, k]).wait()


def gather_gram(frames):
    lines, own, columns = frames.shape
    elevs = own * Z * X
    chunks = (lines - sum(LAST)) // STEP + len(LAST)
    plane = Z * X
    shard = 1280 // (2 * plane)
    return pl.pallas_call(
        gather_gram_kernel,
        out_shape=(
            jax.ShapeDtypeStruct((lines, elevs, LANES), jnp.float32),
            jax.ShapeDtypeStruct((2 * plane, shard, LANES), jnp.float32),
        ),
        in_specs=[pl.BlockSpec(memory_space=pl.ANY)],
        out_specs=(pl.BlockSpec(memory_space=pl.ANY), pl.BlockSpec(memory_space=pltpu.VMEM)),
        scratch_shapes=[
            pltpu.VMEM((lines, elevs, LANES), jnp.float32),
            pltpu.VMEM((3, 256, 256), jnp.float32),
            pltpu.VMEM((2 * plane, shard, LANES), jnp.float32),
            pltpu.VMEM((plane, shard, LANES), jnp.float32),
            pltpu.VMEM((plane, shard, LANES), jnp.float32),
            pltpu.VMEM((plane, shard, LANES), jnp.float32),
            pltpu.VMEM((shard, LANES), jnp.float32),
            pltpu.VMEM((4, shard, LANES), jnp.float32),
            pltpu.VMEM((shard, LANES), jnp.float32),
            pltpu.VMEM((plane, shard, LANES), jnp.float32),
            pltpu.SemaphoreType.DMA((chunks,)),
            pltpu.SemaphoreType.DMA((chunks,)),
            pltpu.SemaphoreType.DMA((5, len(PARTS))),
            pltpu.SemaphoreType.DMA((5, len(PARTS))),
            pltpu.SemaphoreType.DMA((chunks,)),
        ],
        compiler_params=pltpu.CompilerParams(
            collective_id=0, has_side_effects=True, vmem_limit_bytes=48 * 1024 * 1024
        ),
        cost_estimate=pl.CostEstimate(
            flops=2 * lines * LANES * elevs * elevs, bytes_accessed=3 * frames.size * 4, transcendentals=0
        ),
        name="gather_gram",
    )(frames)


def iota(shape, dim):
    return lax.broadcasted_iota(jnp.int32, shape, dim)


def dot_nn(a, b):
    return jnp.dot(a, b, precision=HIGHEST, preferred_element_type=jnp.float32)


def split(v):
    high = v.astype(jnp.bfloat16)
    return high, (v - high.astype(jnp.float32)).astype(jnp.bfloat16)


def cholesky_inverse(m):
    n = m.shape[0]
    tiles = n // 8
    sub, lane = iota((8, n), 0), iota((8, n), 1)

    def up(row):
        return jnp.broadcast_to(row, (8, n))

    def along(tile, j):
        return jnp.broadcast_to(tile[:, j : j + 1], (8, n))

    a = [m[8 * i : 8 * i + 8, :] for i in range(tiles)]
    out = []
    diagonal = [along(a[0], t) for t in range(8)]
    for p in range(tiles):
        j = 8 * p
        columns = [[along(a[i], j + t) for i in range(p + 1, tiles)] for t in range(8)]
        ahead = [along(a[p + 1], j + 8 + s) for s in range(8)] if p + 1 < tiles else []
        panel = (lane >= j) & (lane < j + 8)
        row = jnp.where(panel, jnp.where(lane == sub + j, 1.0, 0.0), a[p])
        below = [jnp.where(panel, 0.0, a[i]) for i in range(p + 1, tiles)]
        pivots = diagonal[0]
        for t in range(8):
            pivot = up(diagonal[t][t : t + 1, :])
            inverse = 1.0 / pivot
            if t:
                pivots = jnp.where(sub == t, pivot, pivots)
            g = jnp.where(sub > t, diagonal[t] * inverse, 0.0)
            f = [q * inverse for q in columns[t]]
            for s in range(t + 1, 8):
                scale = up(diagonal[t][s : s + 1, :])
                diagonal[s] = diagonal[s] - g * scale
                columns[s] = [q - h * scale for q, h in zip(columns[s], f)]
            ahead = [q - f[0] * up(columns[t][0][s : s + 1, :]) for s, q in enumerate(ahead)]
            pivot_row = up(row[t : t + 1, :])
            row = row - g * pivot_row
            below = [q - h * pivot_row for q, h in zip(below, f)]
        a = a[: p + 1] + below
        diagonal = ahead
        out.append(jnp.where(lane < j + 8, row, 0.0) * lax.rsqrt(pivots))
    return jnp.concatenate(out, axis=0)


def split3(v):
    high = v.astype(jnp.bfloat16)
    rest = v - high.astype(jnp.float32)
    middle = rest.astype(jnp.bfloat16)
    return high, middle, (rest - middle.astype(jnp.float32)).astype(jnp.bfloat16)


def dot_parts(a, b):
    rows = a.shape[0]
    a = split3(a)
    first = jnp.dot(jnp.concatenate(a, axis=0), b[0][...], preferred_element_type=jnp.float32)
    second = jnp.dot(jnp.concatenate(a[:2], axis=0), b[1][...], preferred_element_type=jnp.float32)
    third = jnp.dot(a[0], b[2][...], preferred_element_type=jnp.float32)
    return first[:rows] + (first[rows : 2 * rows] + second[:rows] + (first[2 * rows :] + second[rows:] + third))


def near_identity(m):
    row, column = iota(m.shape, 0), iota(m.shape, 1)
    e = m - jnp.where(row == column, 1.0, 0.0)
    lower = jnp.where(row > column, e, jnp.where(row == column, 0.5 * e, 0.0))
    return jnp.sum(e * e) <= 3e-8, lower.astype(jnp.bfloat16)


def basis_core_kernel(x, packed, start, core, basis_out, buf, first, out, turned, wide, gh, gm, gl, in_sem, start_sem, out_sem):
    chunks = x.shape[0] // CORE_STEP

    def load(c):
        rows = pl.ds(c * CORE_STEP, CORE_STEP)
        return pltpu.make_async_copy(x.at[rows], buf.at[rows], in_sem.at[c])

    def store(c):
        rows = pl.ds(c * CORE_STEP, CORE_STEP)
        return pltpu.make_async_copy(out.at[rows], core.at[rows], out_sem.at[c])

    begin = pltpu.make_async_copy(start, first, start_sem)
    begin.start()
    for c in range(chunks):
        load(c).start()

    places = [(0, 0), (1, 0), (1, 1), (2, 0), (2, 1), (3, 0), (3, 1), (2, 2), (3, 2), (3, 3)]
    for n, (i, j) in enumerate(places):
        tile = packed[pl.ds(n * 128, 128), :]
        for part, value in zip((gh, gm, gl), split3(tile)):
            part[pl.ds(i * 128, 128), pl.ds(j * 128, 128)] = value
        if i != j:
            for part, value in zip((gh, gm, gl), split3(tile.T)):
                part[pl.ds(j * 128, 128), pl.ds(i * 128, 128)] = value

    begin.wait()
    wide[...] = dot_parts(first[...], (gh, gm, gl))

    def turn(last):
        w = wide[...]
        w = dot_nn(cholesky_inverse(dot_nt(w, w)), w)
        m = dot_nt(w, w)
        near, lower = near_identity(m)

        def corrected(v):
            return v - jnp.dot(lower, v.astype(jnp.bfloat16), preferred_element_type=jnp.float32)

        if last:
            first[...] = corrected(w)
        else:
            wide[...] = corrected(dot_parts(w, (gh, gm, gl)))

        @pl.when(jnp.logical_not(near))
        def _():
            first[...] = dot_nn(cholesky_inverse(m), w)
            if not last:
                wide[...] = dot_parts(first[...], (gh, gm, gl))

    def earlier_turn(_, carry):
        turn(False)
        return carry

    lax.fori_loop(0, ITERS - 1, earlier_turn, 0)
    turn(True)
    basis = first[...]
    high, low = split(basis)
    both = jnp.concatenate([high, low], axis=0)
    kept = basis.shape[0]

    for c in range(chunks):
        load(c).wait()

    def project(c, _):
        for i in range(0, CORE_STEP, 2):
            l = c * CORE_STEP + i
            xh, xl = split(jnp.concatenate([buf[l], buf[l + 1]], axis=1))
            r = jnp.dot(both, xh, preferred_element_type=jnp.float32)
            q = jnp.dot(high, xl, preferred_element_type=jnp.float32)
            s = r[:kept] + (r[kept:] + q)
            out[l] = s[:, :LANES]
            out[l + 1] = s[:, LANES:]
        store(c).start()
        return 0

    lax.fori_loop(0, chunks, project, 0)

    turned[...] = basis.T
    own = basis_out.shape[0]
    basis_out[...] = turned[pl.ds(pl.multiple_of(lax.axis_index("elev") * own, 8), own), :]

    def drain(c, _):
        store(c).wait()
        return 0

    lax.fori_loop(0, chunks, drain, 0)


def basis_core(x, packed, start, own):
    lines, elevs, lanes = x.shape
    kept = start.shape[0]
    chunks = lines // CORE_STEP
    return pl.pallas_call(
        basis_core_kernel,
        out_shape=(
            jax.ShapeDtypeStruct((lines, kept, lanes), jnp.float32),
            jax.ShapeDtypeStruct((own, kept), jnp.float32),
        ),
        in_specs=[pl.BlockSpec(memory_space=p) for p in (pl.ANY, pltpu.VMEM, pl.ANY)],
        out_specs=(pl.BlockSpec(memory_space=pl.ANY), pl.BlockSpec(memory_space=pltpu.VMEM)),
        scratch_shapes=[
            pltpu.VMEM((lines, elevs, lanes), jnp.float32),
            pltpu.VMEM((kept, elevs), jnp.float32),
            pltpu.VMEM((lines, kept, lanes), jnp.float32),
            pltpu.VMEM((elevs, kept), jnp.float32),
            pltpu.VMEM((kept, elevs), jnp.float32),
            pltpu.VMEM((elevs, elevs), jnp.bfloat16),
            pltpu.VMEM((elevs, elevs), jnp.bfloat16),
            pltpu.VMEM((elevs, elevs), jnp.bfloat16),
            pltpu.SemaphoreType.DMA((chunks,)),
            pltpu.SemaphoreType.DMA,
            pltpu.SemaphoreType.DMA((chunks,)),
        ],
        compiler_params=pltpu.CompilerParams(vmem_limit_bytes=48 * 1024 * 1024),
        cost_estimate=pl.CostEstimate(
            flops=6 * lines * lanes * elevs * kept, bytes_accessed=2 * x.size * 4, transcendentals=0
        ),
        name="basis_core",
    )(x, packed, start)


def per_device(frames, start_basis):
    regrouped, packed = gather_gram(frames)
    return basis_core(regrouped, packed.reshape(-1, LANES), start_basis.T, frames.shape[1])


def solution(mesh):
    return jax.shard_map(
        per_device,
        mesh=mesh,
        in_specs=(P("lat", "elev", None), P()),
        out_specs=(P("lat", None, "elev"), P("elev", None)),
        check_vma=False,
    )
```

```python
import functools

import jax
import jax.numpy as jnp
from jax import lax
from jax.experimental import pallas as pl
from jax.experimental.pallas import tpu as pltpu
from jax.sharding import PartitionSpec as P

ITERS = 3
HIGHEST = lax.Precision.HIGHEST
LANES = 128
STEP = 4
CORE_STEP = 16
STORE = 4
Z = 4
X = 4
PARTS = ((0, 24), (24, 16))


def dot_nt(a, b):
    return lax.dot_general(
        a, b, (((1,), (1,)), ((), ())), precision=HIGHEST, preferred_element_type=jnp.float32
    )


def hops(offset):
    return min(offset[0], Z - offset[0]) + min(offset[1], X - offset[1])


def gather_gram_kernel(
    frames, x_out, g_out, buf, gacc, packed, half_in, half, ring_in, part, y_in, total, half_all,
    recv, send, ar_recv, ar_send, out_sem,
):
    lines = frames.shape[0]
    own = frames.shape[1]
    chunks = lines // STEP
    lat = lax.axis_index("lat")
    elev = lax.axis_index("elev")
    core = lax.rem(lat, 2)
    y = lat // 2
    x = lax.rem(elev, X)
    z = elev // X
    partner = lat + 1 - 2 * core
    offsets = sorted([(dz, dx) for dz in range(Z) for dx in range(X) if dz or dx], key=hops)
    far_first = [lax.rem(z + dz, Z) * X + lax.rem(x + dx, X) for dz, dx in reversed(offsets)]
    peers = []
    for n in range(len(far_first)):
        peers.append(far_first[n // 2] if n % 2 else far_first[len(far_first) - 1 - n // 2])
    y_peers = [lax.rem(y + dy, 4) * 2 + core for dy in (2, 1, 3)]

    barrier = pltpu.get_barrier_semaphore()
    for p in peers:
        pl.semaphore_signal(barrier, inc=1, device_id={"elev": p}, device_id_type=pl.DeviceIdType.MESH)
    for q in y_peers + [partner]:
        pl.semaphore_signal(barrier, inc=1, device_id={"lat": q}, device_id_type=pl.DeviceIdType.MESH)
    pl.semaphore_wait(barrier, len(peers) + len(y_peers) + 1)

    gacc[...] = jnp.zeros_like(gacc)
    mine = pl.ds(pl.multiple_of(elev * own, own), own)

    def issue(c, _):
        rows = pl.ds(c * STEP, STEP)
        for p in peers:
            pltpu.make_async_remote_copy(
                src_ref=frames.at[rows, :, pl.ds(pl.multiple_of(p * LANES, LANES), LANES)],
                dst_ref=buf.at[rows, mine, :],
                send_sem=send.at[c],
                recv_sem=recv.at[c],
                device_id={"elev": p},
                device_id_type=pl.DeviceIdType.MESH,
            ).start()
        pltpu.make_async_copy(
            frames.at[rows, :, pl.ds(pl.multiple_of(elev * LANES, LANES), LANES)],
            buf.at[rows, mine, :],
            recv.at[c],
        ).start()
        return 0

    lax.fori_loop(0, chunks, issue, 0)

    def consume(c, _):
        rows = pl.ds(c * STEP, STEP)
        pltpu.make_async_copy(buf.at[rows], buf.at[rows], recv.at[c]).wait()
        pltpu.make_async_copy(buf.at[rows], x_out.at[rows], out_sem.at[c]).start()
        block = jnp.concatenate([buf[c * STEP + i] for i in range(STEP)], axis=1)
        low, high = block[:256], block[256:]
        gacc[0] += dot_nt(low, low)
        gacc[1] += dot_nt(high, low)
        gacc[2] += dot_nt(high, high)
        return 0

    lax.fori_loop(0, chunks, consume, 0)

    places = [(0, 0, 0), (0, 1, 0), (0, 1, 1), (1, 0, 0), (1, 0, 1), (1, 1, 0), (1, 1, 1), (2, 0, 0), (2, 1, 0), (2, 1, 1)]
    blocks = [gacc[g, pl.ds(i * 128, 128), pl.ds(j * 128, 128)] for g, i, j in places]
    packed[...] = jnp.concatenate(blocks, axis=0).reshape(packed.shape)

    plane = Z * X
    parts = [(k, pl.ds(first, count)) for k, (first, count) in enumerate(PARTS)]
    kept = pl.ds(core * plane, plane)
    given = pl.ds((1 - core) * plane, plane)

    def to_partner(src, dst, hop, k):
        return pltpu.make_async_remote_copy(
            src_ref=src,
            dst_ref=dst,
            send_sem=ar_send.at[hop, k],
            recv_sem=ar_recv.at[hop, k],
            device_id={"lat": partner},
            device_id_type=pl.DeviceIdType.MESH,
        )

    def send_all(src_of, dst, axis, targets, hop, k, mine_src):
        for p in targets:
            pltpu.make_async_remote_copy(
                src_ref=src_of(p),
                dst_ref=dst,
                send_sem=ar_send.at[hop, k],
                recv_sem=ar_recv.at[hop, k],
                device_id={axis: p},
                device_id_type=pl.DeviceIdType.MESH,
            ).start()
        pltpu.make_async_copy(mine_src, dst, ar_recv.at[hop, k]).start()

    swaps = [to_partner(packed.at[given, rows], half_in.at[:, rows], 0, k) for k, rows in parts]
    for swap in swaps:
        swap.start()
    for k, rows in parts:
        swaps[k].wait()
        half[:, rows] = packed[kept, rows] + half_in[:, rows]
        send_all(lambda p: half.at[p, rows], ring_in.at[elev, rows], "elev", far_first, 1, k, half.at[elev, rows])
    def drain(c, _):
        rows = pl.ds(c * STEP, STEP)
        gone = buf.at[rows, pl.ds(0, (plane - 1) * own), :]
        pltpu.make_async_copy(gone, gone, send.at[c]).wait()
        pltpu.make_async_copy(buf.at[rows], x_out.at[rows], out_sem.at[c]).wait()
        return 0

    lax.fori_loop(0, chunks, drain, 0)

    for k, rows in parts:
        pltpu.make_async_copy(ring_in.at[:, rows], ring_in.at[:, rows], ar_recv.at[1, k]).wait()
        part[rows] = jnp.sum(ring_in[:, rows], axis=0)
        send_all(lambda q: part.at[rows], y_in.at[y, rows], "lat", y_peers, 2, k, part.at[rows])
    for k, rows in parts:
        pltpu.make_async_copy(y_in.at[:, rows], y_in.at[:, rows], ar_recv.at[2, k]).wait()
        total[rows] = (y_in[0, rows] + y_in[1, rows]) + (y_in[2, rows] + y_in[3, rows])
        send_all(lambda p: total.at[rows], half_all.at[elev, rows], "elev", far_first, 3, k, total.at[rows])
    swaps = [to_partner(half_all.at[:, rows], g_out.at[kept, rows], 4, k) for k, rows in parts]
    for k, rows in parts:
        pltpu.make_async_copy(half_all.at[:, rows], half_all.at[:, rows], ar_recv.at[3, k]).wait()
        swaps[k].start()
        g_out[kept, rows] = half_all[:, rows]
    for swap in swaps:
        swap.wait()

    n = plane - 1
    for k, rows in parts:
        for hop, gone in ((1, half.at[pl.ds(0, n), rows]), (2, y_in.at[pl.ds(0, 3), rows]), (3, half.at[pl.ds(0, n), rows])):
            pltpu.make_async_copy(gone, gone, ar_send.at[hop, k]).wait()


def gather_gram(frames):
    lines, own, columns = frames.shape
    elevs = own * Z * X
    chunks = lines // STEP
    plane = Z * X
    shard = 1280 // (2 * plane)
    return pl.pallas_call(
        gather_gram_kernel,
        out_shape=(
            jax.ShapeDtypeStruct((lines, elevs, LANES), jnp.float32),
            jax.ShapeDtypeStruct((2 * plane, shard, LANES), jnp.float32),
        ),
        in_specs=[pl.BlockSpec(memory_space=pl.ANY)],
        out_specs=(pl.BlockSpec(memory_space=pl.ANY), pl.BlockSpec(memory_space=pltpu.VMEM)),
        scratch_shapes=[
            pltpu.VMEM((lines, elevs, LANES), jnp.float32),
            pltpu.VMEM((3, 256, 256), jnp.float32),
            pltpu.VMEM((2 * plane, shard, LANES), jnp.float32),
            pltpu.VMEM((plane, shard, LANES), jnp.float32),
            pltpu.VMEM((plane, shard, LANES), jnp.float32),
            pltpu.VMEM((plane, shard, LANES), jnp.float32),
            pltpu.VMEM((shard, LANES), jnp.float32),
            pltpu.VMEM((4, shard, LANES), jnp.float32),
            pltpu.VMEM((shard, LANES), jnp.float32),
            pltpu.VMEM((plane, shard, LANES), jnp.float32),
            pltpu.SemaphoreType.DMA((chunks,)),
            pltpu.SemaphoreType.DMA((chunks,)),
            pltpu.SemaphoreType.DMA((5, len(PARTS))),
            pltpu.SemaphoreType.DMA((5, len(PARTS))),
            pltpu.SemaphoreType.DMA((chunks,)),
        ],
        compiler_params=pltpu.CompilerParams(
            collective_id=0, has_side_effects=True, vmem_limit_bytes=48 * 1024 * 1024
        ),
        cost_estimate=pl.CostEstimate(
            flops=2 * lines * LANES * elevs * elevs, bytes_accessed=3 * frames.size * 4, transcendentals=0
        ),
        name="gather_gram",
    )(frames)


def iota(shape, dim):
    return lax.broadcasted_iota(jnp.int32, shape, dim)


def dot_nn(a, b):
    return jnp.dot(a, b, precision=HIGHEST, preferred_element_type=jnp.float32)


def split(v):
    high = v.astype(jnp.bfloat16)
    return high, (v - high.astype(jnp.float32)).astype(jnp.bfloat16)


def cholesky_inverse(m):
    n = m.shape[0]
    tiles = n // 8
    sub, lane = iota((8, n), 0), iota((8, n), 1)

    def up(row):
        return jnp.broadcast_to(row, (8, n))

    def along(tile, j):
        return jnp.broadcast_to(tile[:, j : j + 1], (8, n))

    a = [m[8 * i : 8 * i + 8, :] for i in range(tiles)]
    out = []
    diagonal = [along(a[0], t) for t in range(8)]
    for p in range(tiles):
        j = 8 * p
        columns = [[along(a[i], j + t) for i in range(p + 1, tiles)] for t in range(8)]
        ahead = [along(a[p + 1], j + 8 + s) for s in range(8)] if p + 1 < tiles else []
        panel = (lane >= j) & (lane < j + 8)
        row = jnp.where(panel, jnp.where(lane == sub + j, 1.0, 0.0), a[p])
        below = [jnp.where(panel, 0.0, a[i]) for i in range(p + 1, tiles)]
        pivots = diagonal[0]
        for t in range(8):
            pivot = up(diagonal[t][t : t + 1, :])
            inverse = 1.0 / pivot
            if t:
                pivots = jnp.where(sub == t, pivot, pivots)
            g = jnp.where(sub > t, diagonal[t] * inverse, 0.0)
            f = [q * inverse for q in columns[t]]
            for s in range(t + 1, 8):
                scale = up(diagonal[t][s : s + 1, :])
                diagonal[s] = diagonal[s] - g * scale
                columns[s] = [q - h * scale for q, h in zip(columns[s], f)]
            ahead = [q - f[0] * up(columns[t][0][s : s + 1, :]) for s, q in enumerate(ahead)]
            pivot_row = up(row[t : t + 1, :])
            row = row - g * pivot_row
            below = [q - h * pivot_row for q, h in zip(below, f)]
        a = a[: p + 1] + below
        diagonal = ahead
        out.append(jnp.where(lane < j + 8, row, 0.0) * lax.rsqrt(pivots))
    return jnp.concatenate(out, axis=0)


def split3(v):
    high = v.astype(jnp.bfloat16)
    rest = v - high.astype(jnp.float32)
    middle = rest.astype(jnp.bfloat16)
    return high, middle, (rest - middle.astype(jnp.float32)).astype(jnp.bfloat16)


def dot_parts(a, b):
    rows = a.shape[0]
    a = split3(a)
    first = jnp.dot(jnp.concatenate(a, axis=0), b[0][...], preferred_element_type=jnp.float32)
    second = jnp.dot(jnp.concatenate(a[:2], axis=0), b[1][...], preferred_element_type=jnp.float32)
    third = jnp.dot(a[0], b[2][...], preferred_element_type=jnp.float32)
    return first[:rows] + (first[rows : 2 * rows] + second[:rows] + (first[2 * rows :] + second[rows:] + third))


def near_identity(m):
    row, column = iota(m.shape, 0), iota(m.shape, 1)
    e = m - jnp.where(row == column, 1.0, 0.0)
    lower = jnp.where(row > column, e, jnp.where(row == column, 0.5 * e, 0.0))
    return jnp.sum(e * e) <= 3e-8, lower.astype(jnp.bfloat16)


def basis_core_kernel(x, packed, start, core, basis_out, buf, first, gram, out, turned, wide, gh, gm, gl, in_sem, start_sem, out_sem):
    chunks = x.shape[0] // CORE_STEP

    def load(c):
        rows = pl.ds(c * CORE_STEP, CORE_STEP)
        return pltpu.make_async_copy(x.at[rows], buf.at[rows], in_sem.at[c])

    def store(c):
        rows = pl.ds(c * STORE, STORE)
        return pltpu.make_async_copy(out.at[rows], core.at[rows], out_sem.at[c])

    begin = pltpu.make_async_copy(start, first, start_sem)
    begin.start()
    for c in range(chunks):
        load(c).start()

    places = [(0, 0), (1, 0), (1, 1), (2, 0), (2, 1), (3, 0), (3, 1), (2, 2), (3, 2), (3, 3)]
    for n, (i, j) in enumerate(places):
        tile = packed[pl.ds(n * 128, 128), :]
        gram[pl.ds(i * 128, 128), pl.ds(j * 128, 128)] = tile
        if i != j:
            gram[pl.ds(j * 128, 128), pl.ds(i * 128, 128)] = tile.T

    for part, value in zip((gh, gm, gl), split3(gram[...])):
        part[...] = value

    begin.wait()
    wide[...] = dot_parts(first[...], (gh, gm, gl))

    def turn(last):
        w = wide[...]
        w = dot_nn(cholesky_inverse(dot_nt(w, w)), w)
        m = dot_nt(w, w)
        near, lower = near_identity(m)

        def corrected(v):
            return v - jnp.dot(lower, v.astype(jnp.bfloat16), preferred_element_type=jnp.float32)

        if last:
            first[...] = corrected(w)
        else:
            wide[...] = corrected(dot_parts(w, (gh, gm, gl)))

        @pl.when(jnp.logical_not(near))
        def _():
            first[...] = dot_nn(cholesky_inverse(m), w)
            if not last:
                wide[...] = dot_parts(first[...], (gh, gm, gl))

    def earlier_turn(_, carry):
        turn(False)
        return carry

    lax.fori_loop(0, ITERS - 1, earlier_turn, 0)
    turn(True)
    basis = first[...]
    turned[...] = basis.T
    own = basis_out.shape[0]
    basis_out[...] = turned[pl.ds(pl.multiple_of(lax.axis_index("elev") * own, 8), own), :]

    high, low = split(basis)
    both = jnp.concatenate([high, low], axis=0)
    kept = basis.shape[0]

    for c in range(chunks):
        load(c).wait()

    def project(c, _):
        for i in range(0, CORE_STEP, 2):
            l = c * CORE_STEP + i
            xh, xl = split(jnp.concatenate([buf[l], buf[l + 1]], axis=1))
            r = jnp.dot(both, xh, preferred_element_type=jnp.float32)
            q = jnp.dot(high, xl, preferred_element_type=jnp.float32)
            s = r[:kept] + (r[kept:] + q)
            out[l] = s[:, :LANES]
            out[l + 1] = s[:, LANES:]
            if (i + 2) % STORE == 0:
                store(c * (CORE_STEP // STORE) + i // STORE).start()
        return 0

    lax.fori_loop(0, chunks, project, 0)

    def drain(c, _):
        store(c).wait()
        return 0

    lax.fori_loop(0, x.shape[0] // STORE, drain, 0)


def basis_core(x, packed, start, own):
    lines, elevs, lanes = x.shape
    kept = start.shape[0]
    chunks = lines // CORE_STEP
    return pl.pallas_call(
        basis_core_kernel,
        out_shape=(
            jax.ShapeDtypeStruct((lines, kept, lanes), jnp.float32),
            jax.ShapeDtypeStruct((own, kept), jnp.float32),
        ),
        in_specs=[pl.BlockSpec(memory_space=p) for p in (pl.ANY, pltpu.VMEM, pl.ANY)],
        out_specs=(pl.BlockSpec(memory_space=pl.ANY), pl.BlockSpec(memory_space=pltpu.VMEM)),
        scratch_shapes=[
            pltpu.VMEM((lines, elevs, lanes), jnp.float32),
            pltpu.VMEM((kept, elevs), jnp.float32),
            pltpu.VMEM((elevs, elevs), jnp.float32),
            pltpu.VMEM((lines, kept, lanes), jnp.float32),
            pltpu.VMEM((elevs, kept), jnp.float32),
            pltpu.VMEM((kept, elevs), jnp.float32),
            pltpu.VMEM((elevs, elevs), jnp.bfloat16),
            pltpu.VMEM((elevs, elevs), jnp.bfloat16),
            pltpu.VMEM((elevs, elevs), jnp.bfloat16),
            pltpu.SemaphoreType.DMA((chunks,)),
            pltpu.SemaphoreType.DMA,
            pltpu.SemaphoreType.DMA((lines // STORE,)),
        ],
        compiler_params=pltpu.CompilerParams(vmem_limit_bytes=48 * 1024 * 1024),
        cost_estimate=pl.CostEstimate(
            flops=6 * lines * lanes * elevs * kept, bytes_accessed=2 * x.size * 4, transcendentals=0
        ),
        name="basis_core",
    )(x, packed, start)


def per_device(frames, start_basis):
    regrouped, packed = gather_gram(frames)
    return basis_core(regrouped, packed.reshape(-1, LANES), start_basis.T, frames.shape[1])


def solution(mesh):
    return jax.shard_map(
        per_device,
        mesh=mesh,
        in_specs=(P("lat", "elev", None), P()),
        out_specs=(P("lat", None, "elev"), P("elev", None)),
        check_vma=False,
    )
```
